32 devices in a mesh: gx: 4 (over x, core), gy: 8 (over z, y).
Axes of the slice: x: 2, y: 2, z: 4, core: 2. Of those that a mesh axis runs over, the one named last changes fastest.
Arguments:
- state: float32 [48, 256, 2048], P(None, 'gx', 'gy'), may hold values from -6 to 6
- right_side: float32 [48, 256, 2048], P(None, 'gx', 'gy'), may hold values from -6 to 6
- sigma: float32 [256, 2048], P('gx', 'gy'), may hold values from 0.25 to 4
- coupling: float32 [6, 6], replicated, may hold values from -2 to 2
- omega: float32 [4], replicated, may hold values from 0.1 to 8
- pressure_coef: float32 [6], replicated, may hold values from 0.5 to 1.5
- tile_cells: int32 [8192, 128], P(('gx', 'gy')), may hold values from 0 to 16383
- tile_owner: int32 [8192, 1], P(('gx', 'gy')), may hold values from 0 to 7; in each aligned block of 256 rows (0 to 255, 256 to 511, ...) at most 48 rows name the same one
- tile_panel: int32 [8192, 1], P(('gx', 'gy')), may hold values from 0 to 31
- interp: float32 [8192, 128, 128], P(('gx', 'gy')), may hold values from -1 to 1
- correction: float32 [32768], P('gy'), may hold values from 0.5 to 2
- mode_shape: float32 [32, 32768], P(None, 'gy'), may hold values from -1 to 1
Outputs:
- new_state: float32 [48, 256, 2048], P(None, 'gx', 'gy')
- panel_pressure: float32 [8, 32768], P(None, 'gy')
- gaf: float32 [32, 8], P('gy')
The draws below stay inside these ranges and needn't reach their ends.
Inputs may be any that keep to these rules, and one draw needn't show every extreme that they name: `tile_owner`: each device's 256 tiles name one owner at most 48 times, a bound that some block reaches.
All inputs are finite; a program needn't handle non-finite values.
Results may differ from the reference program's by a relative error of at most 0.0003.
Values sent between devices are 32-bit elements; how exact they have to be, the bound alone decides.
No kernel may reach another device: no remote copies, remote signals or barrier semaphores. Data moves between devices by JAX's collectives and lax.ppermute only.
A program may use at most 192 MiB of HBM per device.

```python
import math
import jax
import jax.numpy as jnp
import numpy as np
from jax import lax

MODES = 4
VARS = 6
SWEEPS = 2
CX = 64
CY = 256
TILES_DEV = 256
PANEL_DEV = 4096
CAP = 48
COMP = 48
NX = 256
NY = 2048
TILES = 8192
OWNERS = 8
PT_DEV = 32
PANELS = 32768
PANEL_TILES = 256
NSM = 32
N_GX = 4
N_GY = 8


def scaled_values(key, shape, fan):
    base_key = jax.random.fold_in(key, 0)
    values = jnp.clip(jax.random.normal(base_key, shape, jnp.float32), -5.0, 5.0)
    return jnp.clip(values * fan ** (-0.5), -1.0, 1.0)


def draw_interp(key, part):
    key = jax.random.fold_in(key, 11)
    fan = TILES_DEV * N_GX * 128 * 128 // PANEL_DEV
    return scaled_values(key, (TILES, 128, 128), float(fan))


def draw_mode_shape(key, part):
    key = jax.random.fold_in(key, 23)
    return scaled_values(key, (NSM, PANELS), float(PANELS))


def set_ends(drawn, key, least, largest):
    longest = drawn.shape.index(max(drawn.shape))
    spots = []
    for shift in (0, 1):
        where = [jax.random.randint(jax.random.fold_in(key, axis), (), 0, length) for axis, length in enumerate(drawn.shape)]
        where[longest] = (where[longest] + shift) % drawn.shape[longest]
        spots.append(tuple(where))
    return drawn.at[spots[0]].set(least).at[spots[1]].set(largest)


def levels(rng, shape, cuts, smallest, top_value):
    loudness = 1.0
    for position, shards_of in cuts:
        steps = jax.random.uniform(jax.random.fold_in(jax.random.fold_in(rng, 6), position), (shards_of,), jnp.float32, smallest / len(cuts), top_value / len(cuts))
        loudness = loudness * jnp.repeat(jnp.exp(steps), shape[position] // shards_of).reshape((-1,) + (1,) * (len(shape) - 1 - position))
    return loudness


def routed_block(stream_key, own, number, rows, count, top, reach, slope):
    order = jax.random.permutation(stream_key, count)
    packed, ordinary = shares(count, rows * top, reach, slope, True), shares(count, rows * top, reach, slope, False)
    places = jnp.arange(count)

    def named(tallies, rotation):
        used = int((tallies > 0).sum())
        fixed = max(1, used // 4)
        moved = fixed + (places - fixed + rotation * (used - fixed)) % max(1, count - fixed)
        return jnp.zeros((count,), jnp.int32).at[order[jnp.where(places < fixed, places, moved)]].set(jnp.asarray(tallies, jnp.int32))

    tallies = jnp.where(number % 4 == 0, named(packed, number // 4), named(ordinary, number - number // 4 - 1))
    mixed = jax.random.permutation(jax.random.fold_in(own, 3), count)
    source_of, receiver = mixed[0:count // 2 * 2:2], mixed[1:count // 2 * 2:2]
    margin = jnp.minimum(tallies[source_of] - 1, reach - tallies[receiver]) // 2
    margin = jnp.where((source_of == order[0]) | (receiver == order[0]) | (tallies[receiver] == 0), 0, jnp.maximum(margin, 0))
    moved = jax.random.randint(jax.random.fold_in(own, 4), (count // 2,), 0, 1 << 20) % (margin + 1)
    tallies = tallies.at[source_of].add(-moved).at[receiver].add(moved)
    members = jnp.searchsorted(jnp.cumsum(tallies), jnp.arange(rows * top), side="right").astype(jnp.int32)
    listing = members.reshape(top, rows).T
    listing = listing[jax.random.permutation(jax.random.fold_in(own, 1), rows)]
    rotation = jax.random.randint(jax.random.fold_in(own, 2), (rows, 1), 0, top)
    return jnp.take_along_axis(listing, (jnp.arange(top)[None, :] + rotation) % top, axis=1)


def shares(number_of, total, bound, skew, full):
    weights = [(1 << 20) // math.isqrt(rank ** skew) + 1 for rank in range(1, number_of + 1)]
    largest = bound if full else min(bound, max(-(-total // number_of), total * weights[0] // sum(weights)))
    least = 1 if total - largest >= number_of - 1 else 0
    given, surplus = [largest] + [least] * (number_of - 1), total - largest - least * (number_of - 1)
    while surplus > 0:
        movable = [i for i in range(1, number_of) if given[i] < largest] or [i for i in range(1, number_of) if given[i] < bound]
        whole, budget = sum([weights[i] for i in movable]), surplus
        for i in movable:
            more = min(bound - given[i], max(1, budget * weights[i] // whole), surplus)
            given[i] = given[i] + more
            surplus = surplus - more
    return np.array(given)


def scatter_about(stream_key, shape, spread, bound, cuts=(), held_as=jnp.bfloat16):
    result = jax.random.normal(stream_key, shape, jnp.float32) * spread
    if len(cuts) > 0:
        result = levels(stream_key, shape, cuts, -0.22, 0.18) * result
    return jnp.clip(result, min=-bound, max=bound).astype(held_as)


def setup_inputs(seed: int = 0) -> dict:
    splits = jax.random.split(jax.random.key(seed), 13)
    state = scatter_about(splits[0], (COMP, NX, NY), 1.0, 6.0, ((1, 4), (2, 8)), jnp.float32)
    right_side = scatter_about(splits[1], (COMP, NX, NY), 1.0, 6.0, ((1, 4), (2, 8)), jnp.float32)
    sigma = jnp.clip(jnp.exp(math.log(4.0) - 2.7725887 * jax.random.uniform(splits[2], (NX, NY), jnp.float32) ** levels(splits[2], (NX, NY), ((0, 4), (1, 8)), -0.2, 0.2)), 0.25, 4.0)
    coupling = scatter_about(splits[3], (VARS, VARS), 8 ** -0.5, 2.0, (), jnp.float32)
    omega = jnp.clip(jnp.exp(jax.random.uniform(splits[4], (MODES,), jnp.float32, math.log(0.1), math.log(8.0))), 0.1, 8.0)
    pressure_coef = jnp.clip(jax.random.uniform(splits[5], (VARS,), jnp.float32, 0.5, 1.5), 0.5, 1.5)
    tile_cells = set_ends(jax.random.randint(splits[6], (TILES, 128), 0, CX * CY), jax.random.fold_in(splits[6], 1), 0, (CX * CY) - 1).astype(jnp.int32)
    tile_owner_keys = jax.random.split(jax.random.fold_in(splits[7], 1), TILES // TILES_DEV)
    tile_owner_turns = jax.random.permutation(jax.random.fold_in(splits[7], 3), TILES // TILES_DEV)
    tile_owner = jax.vmap(lambda own, number: routed_block(jax.random.fold_in(splits[7], 2), own, number, TILES_DEV, OWNERS, 1, CAP, 2))(tile_owner_keys, tile_owner_turns).reshape((TILES, 1))
    tile_panel = set_ends(jax.random.randint(splits[8], (TILES, 1), 0, PT_DEV), jax.random.fold_in(splits[8], 1), 0, PT_DEV - 1).astype(jnp.int32)
    interp = draw_interp(jax.random.fold_in(splits[12], 71), 0)
    correction = jnp.clip(jnp.exp(math.log(2.0) - 1.3862944 * jax.random.uniform(splits[10], (PANELS,), jnp.float32) ** levels(splits[10], (PANELS,), ((0, 8),), -0.2, 0.2)), 0.5, 2.0)
    mode_shape = draw_mode_shape(jax.random.fold_in(splits[12], 71), 0)
    return dict(state=state, right_side=right_side, sigma=sigma, coupling=coupling, omega=omega, pressure_coef=pressure_coef, tile_cells=tile_cells, tile_owner=tile_owner, tile_panel=tile_panel, interp=interp, correction=correction, mode_shape=mode_shape)


def four_sides(field):
    padded = jnp.pad(field, ((0, 0), (0, 0), (1, 1), (1, 1)))
    total = padded[:, :, 2:, 1:-1] + padded[:, :, :-2, 1:-1]
    total = total + padded[:, :, 1:-1, 2:] + padded[:, :, 1:-1, :-2]
    return total


def reference(state, right_side, sigma, coupling, omega, pressure_coef, tile_cells, tile_owner, tile_panel, interp, correction, mode_shape):
    dval = 4.0 + sigma
    field5 = state.reshape(MODES, 2, VARS, NX, NY)
    rhs5 = right_side.reshape(MODES, 2, VARS, NX, NY)

    def one_mode(items):
        field, rhs, freq = items
        for sweep in range(SWEEPS):
            nbs = four_sides(field)
            mixed = jnp.einsum('vw,pwxy->pvxy', coupling, nbs, precision=lax.Precision.HIGHEST)
            a_re = dval * field[0] - mixed[0] - freq * field[1]
            a_im = dval * field[1] - mixed[1] + freq * field[0]
            s_re = rhs[0] - a_re
            s_im = rhs[1] - a_im
            denom = dval * dval + freq * freq
            upd_re = (dval * s_re + freq * s_im) / denom
            upd_im = (dval * s_im - freq * s_re) / denom
            field = field + 0.8 * jnp.stack([upd_re, upd_im], axis=0)
        return field

    relaxed = lax.map(one_mode, (field5, rhs5, omega))
    new_state = relaxed.reshape(COMP, NX, NY)
    press = jnp.einsum('v,mpvxy->mpxy', pressure_coef, relaxed, precision=lax.Precision.HIGHEST)
    press = press.reshape(2 * MODES, NX * NY)

    def block(carry, device):
        start = device * TILES_DEV
        cells = lax.dynamic_slice_in_dim(tile_cells, start, TILES_DEV, 0)
        row_dev = device // N_GY
        col_dev = device % N_GY
        flat = (row_dev * CX + cells // CY) * NY + (col_dev * CY + cells % CY)
        surf = jnp.take(press, flat.reshape(-1), axis=1).reshape(2 * MODES, TILES_DEV, 128)
        weights = lax.dynamic_slice_in_dim(interp, start, TILES_DEV, 0)
        contrib = jnp.einsum('qtc,tcp->tqp', surf, weights, precision=lax.Precision.HIGHEST)
        owner = lax.dynamic_slice_in_dim(tile_owner, start, TILES_DEV, 0)[:, 0]
        panel = lax.dynamic_slice_in_dim(tile_panel, start, TILES_DEV, 0)[:, 0]
        target = (owner * PT_DEV + panel).astype(jnp.int32)
        carry = carry.at[:, target, :].add(jnp.transpose(contrib, (1, 0, 2)))
        return carry, None

    start_sum = jnp.zeros((2 * MODES, PANEL_TILES, 128), jnp.float32)
    devices = jnp.arange(N_GX * N_GY, dtype=jnp.int32)
    summed, unused = lax.scan(block, start_sum, devices)
    panel_pressure = summed.reshape(2 * MODES, PANELS)
    corrected = panel_pressure * correction[None, :]
    gaf = jnp.dot(mode_shape, corrected.T, precision=lax.Precision.HIGHEST)
    return new_state, panel_pressure, gaf
```

```python
import functools

import jax
import jax.numpy as jnp
from jax import lax
from jax.experimental import pallas as pl
from jax.experimental.pallas import tpu as pltpu
from jax.sharding import PartitionSpec as P

F32 = jnp.float32
BF16 = jnp.bfloat16
LANES = 128
BLOCK_TILES = 16
VMEM_LIMIT = 48 << 20


def vmem():
    return pl.BlockSpec(memory_space=pltpu.VMEM)


def smem():
    return pl.BlockSpec(memory_space=pltpu.SMEM)


def pack_edges(field_ref, first, planes, up_ref, down_ref, left_ref, right_ref):
    rows, cols = field_ref.shape[1:]
    lane = lax.broadcasted_iota(jnp.int32, (rows, LANES), 1)
    left = left_ref[...]
    right = right_ref[...]
    for k in range(planes):
        up_ref[0, k : k + 1, :] = field_ref[k, 0:1, :]
        down_ref[0, k : k + 1, :] = field_ref[k, rows - 1 : rows, :]
        here = lane == first + k
        left = jnp.where(here, field_ref[k, :, 0:1], left)
        right = jnp.where(here, field_ref[k, :, cols - 1 : cols], right)
    left_ref[...] = left
    right_ref[...] = right


def pack_kernel(state_ref, up_ref, down_ref, left_ref, right_ref):
    mode = pl.program_id(0)
    planes = state_ref.shape[0]

    @pl.when(mode == 0)
    def _():
        left_ref[...] = jnp.zeros_like(left_ref)
        right_ref[...] = jnp.zeros_like(right_ref)

    pack_edges(state_ref, mode * planes, planes, up_ref, down_ref, left_ref, right_ref)


def sweep_kernel(
    last,
    coupling_ref,
    omega_ref,
    coef_ref,
    state_ref,
    rhs_ref,
    sigma_ref,
    above_ref,
    below_ref,
    west_ref,
    east_ref,
    new_ref,
    *rest,
):
    nbs_ref, a_ref, b_ref, press_ref = rest[-4:]
    mode = pl.program_id(0)
    planes, rows, cols = state_ref.shape
    nvar = planes // 2
    parts = 2 * omega_ref.shape[0]
    freq = omega_ref[mode]
    dval = 4.0 + sigma_ref[...]
    scale = 0.8 / (dval * dval + freq * freq)
    a_ref[...] = dval * scale
    b_ref[...] = freq * scale

    row = lax.broadcasted_iota(jnp.int32, (rows, cols), 0)
    lane = lax.broadcasted_iota(jnp.int32, (rows, LANES), 1)
    for k in range(planes):
        comp = mode * planes + k
        plane = state_ref[k]
        total = jnp.where(row == 0, above_ref[0, k : k + 1, :], pltpu.roll(plane, 1, 0))
        total = total + jnp.where(
            row == rows - 1, below_ref[0, k : k + 1, :], pltpu.roll(plane, rows - 1, 0)
        )
        west = pltpu.roll(west_ref[...], lax.rem(LANES - comp, LANES), 1)
        east = pltpu.roll(east_ref[...], LANES - 1 - comp, 1)
        from_west = pltpu.roll(plane, 1, 1)
        from_east = pltpu.roll(plane, cols - 1, 1)
        nbs_ref[k, :, :LANES] = (
            total[:, :LANES]
            + jnp.where(lane == 0, west, from_west[:, :LANES])
            + from_east[:, :LANES]
        )
        nbs_ref[k, :, cols - LANES :] = (
            total[:, cols - LANES :]
            + from_west[:, cols - LANES :]
            + jnp.where(lane == LANES - 1, east, from_east[:, cols - LANES :])
        )

    weight = [[coupling_ref[v, w] for w in range(nvar)] for v in range(nvar)]
    coef = [coef_ref[v] for v in range(nvar)]

    def strip(step, carry):
        here = pl.ds(pl.multiple_of(step * 8, 8), 8)
        nbs = [nbs_ref[k, here, :] for k in range(planes)]
        a = a_ref[here, :]
        b = b_ref[here, :]
        press_re = press_im = None
        for v in range(nvar):
            res_re = rhs_ref[v, here, :]
            res_im = rhs_ref[nvar + v, here, :]
            for w in range(nvar):
                res_re = res_re + weight[v][w] * nbs[w]
                res_im = res_im + weight[v][w] * nbs[nvar + w]
            new_re = 0.2 * state_ref[v, here, :] + a * res_re + b * res_im
            new_im = 0.2 * state_ref[nvar + v, here, :] + a * res_im - b * res_re
            new_ref[v, here, :] = new_re
            new_ref[nvar + v, here, :] = new_im
            if last:
                press_re = coef[v] * new_re if v == 0 else press_re + coef[v] * new_re
                press_im = coef[v] * new_im if v == 0 else press_im + coef[v] * new_im
        if last:
            for part, value in enumerate((press_re, press_im)):
                start = step * (8 * parts) + 2 * mode + part
                for half in range(cols // LANES):
                    piece = value[:, half * LANES : (half + 1) * LANES]
                    press_ref[half, pl.ds(start, 8, stride=parts), :] = piece
        return carry

    lax.fori_loop(0, rows // 8, strip, 0)
    if last:
        table_ref = rest[0]

        @pl.when(mode == pl.num_programs(0) - 1)
        def _():
            size = table_ref.shape[0] // 2
            for half in range(cols // LANES):
                whole = press_ref[half]
                high = whole.astype(BF16)
                span = slice(half * LANES, (half + 1) * LANES)
                table_ref[:size, span] = high
                table_ref[size:, span] = (whole - high.astype(F32)).astype(BF16)

    else:
        up_ref, down_ref, left_ref, right_ref = rest[:4]

        @pl.when(mode == 0)
        def _():
            left_ref[...] = jnp.zeros_like(left_ref)
            right_ref[...] = jnp.zeros_like(right_ref)

        pack_edges(new_ref, mode * planes, planes, up_ref, down_ref, left_ref, right_ref)


def edge_shapes(modes, planes, rows, cols):
    shapes = (
        jax.ShapeDtypeStruct((modes, planes, cols), F32),
        jax.ShapeDtypeStruct((modes, planes, cols), F32),
        jax.ShapeDtypeStruct((rows, LANES), F32),
        jax.ShapeDtypeStruct((rows, LANES), F32),
    )
    row_spec = pl.BlockSpec((1, planes, cols), lambda m: (m, 0, 0))
    col_spec = pl.BlockSpec((rows, LANES), lambda m: (0, 0))
    return shapes, (row_spec, row_spec, col_spec, col_spec)


def pack(state, modes):
    comp, rows, cols = state.shape
    planes = comp // modes
    shapes, specs = edge_shapes(modes, planes, rows, cols)
    return pl.pallas_call(
        pack_kernel,
        grid=(modes,),
        out_shape=shapes,
        in_specs=[pl.BlockSpec((planes, rows, cols), lambda m: (m, 0, 0))],
        out_specs=specs,
        compiler_params=pltpu.CompilerParams(vmem_limit_bytes=VMEM_LIMIT),
        name="pack",
    )(state)


def exchange(edges):
    up, down, left, right = edges
    nx = lax.axis_size("gx")
    ny = lax.axis_size("gy")
    above = lax.ppermute(down, "gx", [(i, i + 1) for i in range(nx - 1)])
    below = lax.ppermute(up, "gx", [(i + 1, i) for i in range(nx - 1)])
    west = lax.ppermute(right, "gy", [(i, i + 1) for i in range(ny - 1)])
    east = lax.ppermute(left, "gy", [(i + 1, i) for i in range(ny - 1)])
    return above, below, west, east


def sweep(last, coupling, omega, coef, field, rhs, sigma, halo):
    comp, rows, cols = field.shape
    modes = omega.shape[0]
    planes = comp // modes
    edges, edge_specs = edge_shapes(modes, planes, rows, cols)
    block = pl.BlockSpec((planes, rows, cols), lambda m: (m, 0, 0))
    if last:
        table = (4 * modes * rows, cols)
        extra = (jax.ShapeDtypeStruct(table, BF16),)
        extra_specs = (pl.BlockSpec(table, lambda m: (0, 0)),)
    else:
        extra, extra_specs = edges, edge_specs
    return pl.pallas_call(
        functools.partial(sweep_kernel, last),
        grid=(modes,),
        out_shape=(jax.ShapeDtypeStruct(field.shape, F32),) + extra,
        in_specs=[
            smem(),
            smem(),
            smem(),
            block,
            block,
            pl.BlockSpec((rows, cols), lambda m: (0, 0)),
            *edge_specs,
        ],
        out_specs=(block,) + extra_specs,
        scratch_shapes=[
            pltpu.VMEM((planes, rows, cols), F32),
            pltpu.VMEM((rows, cols), F32),
            pltpu.VMEM((rows, cols), F32),
            pltpu.VMEM((cols // LANES, 2 * modes * rows if last else 8, LANES), F32),
        ],
        compiler_params=pltpu.CompilerParams(vmem_limit_bytes=VMEM_LIMIT),
        name="sweep",
    )(coupling, omega, coef, field, rhs, sigma, *halo)


def tile_kernel(place_ref, table_ref, cells_ref, interp_ref, keep_ref, send_ref, acc_ref):
    step = pl.program_id(0)
    block = cells_ref.shape[0]
    parts = acc_ref.shape[1]
    size = table_ref.shape[0] // 2
    cols = table_ref.shape[1]
    rows = size // parts
    shift = cols.bit_length() - 1

    @pl.when(step == 0)
    def _():
        acc_ref[...] = jnp.zeros_like(acc_ref)

    col_at = lax.broadcasted_iota(jnp.int16, (cols, 2 * LANES), 0)
    one = jnp.ones((), BF16)
    zero = jnp.zeros((), BF16)
    blank = jnp.zeros((2 * parts, LANES), F32)
    surfs = []
    for pair in range(block // 2):
        cells = jnp.concatenate(
            [cells_ref[2 * pair : 2 * pair + 1, :], cells_ref[2 * pair + 1 : 2 * pair + 2, :]], axis=1
        )
        col = jnp.broadcast_to((cells & (cols - 1)).astype(jnp.int16), (cols, 2 * LANES))
        hot = jnp.where(col_at == col, one, zero)
        found = jnp.dot(table_ref[...], hot, preferred_element_type=F32)
        found = (found[:size] + found[size:]).reshape(rows, parts, 2 * LANES)
        row = jnp.broadcast_to(cells >> shift, (parts, 2 * LANES))
        bit = rows // 2
        while bit:
            found = jnp.where(((row & bit) != 0)[None], found[bit:], found[:bit])
            bit //= 2
        surfs.append(found[0])
    for pair, surf in enumerate(surfs):
        high = surf.astype(BF16).astype(F32)
        split = jnp.concatenate([high, surf - high], axis=0)
        left = jnp.concatenate(
            [
                jnp.concatenate([split[:, :LANES], blank], axis=1),
                jnp.concatenate([blank, split[:, LANES:]], axis=1),
            ],
            axis=0,
        ).astype(BF16)
        weight = interp_ref[2 * pair : 2 * pair + 2].reshape(2 * LANES, LANES)
        weight_high = weight.astype(BF16)
        weight_low = (weight - weight_high.astype(F32)).astype(BF16)
        right = jnp.concatenate([weight_high, weight_low], axis=1)
        out = jnp.dot(left, right, preferred_element_type=F32)
        for side in range(2):
            line = out[side * 2 * parts : (side + 1) * 2 * parts]
            high_part = line[:parts, :LANES] + line[:parts, LANES:]
            at = place_ref[step * block + 2 * pair + side]
            acc_ref[at] += high_part + line[parts:, :LANES]

    @pl.when(step == pl.num_programs(0) - 1)
    def _():
        half = keep_ref.shape[0]
        keep_ref[...] = acc_ref[:half]
        send_ref[...] = acc_ref[half:]


def tile_sums(place, table, cells, interp, panel_tiles, parts):
    tiles = cells.shape[0]
    half = (panel_tiles // 2, parts, LANES)
    block = min(BLOCK_TILES, tiles)
    return pl.pallas_call(
        tile_kernel,
        grid=(tiles // block,),
        out_shape=(jax.ShapeDtypeStruct(half, F32), jax.ShapeDtypeStruct(half, F32)),
        in_specs=[
            smem(),
            pl.BlockSpec(table.shape, lambda i: (0, 0)),
            pl.BlockSpec((block, LANES), lambda i: (i, 0)),
            pl.BlockSpec((block, LANES, LANES), lambda i: (i, 0, 0)),
        ],
        out_specs=(pl.BlockSpec(half, lambda i: (0, 0, 0)), pl.BlockSpec(half, lambda i: (0, 0, 0))),
        scratch_shapes=[pltpu.VMEM((panel_tiles, parts, LANES), F32)],
        compiler_params=pltpu.CompilerParams(vmem_limit_bytes=VMEM_LIMIT),
        name="tiles",
    )(place, table, cells, interp)


def combine_kernel(order, me_ref, keep_ref, got_ref, shapes_ref, next_keep_ref, next_send_ref):
    owners = len(order)
    chunk = keep_ref.shape[0] // owners
    parts = keep_ref.shape[1]
    modes = shapes_ref.shape[0] // owners
    half = keep_ref.shape[0] // 2
    force = jnp.zeros((parts, modes), F32)
    for at, relative in enumerate(order):
        lines = keep_ref[at * chunk : (at + 1) * chunk] + got_ref[at * chunk : (at + 1) * chunk]
        first = at * chunk
        if first < half:
            next_keep_ref[first : first + chunk] = lines
        else:
            next_send_ref[first - half : first - half + chunk] = lines
        flat = jnp.concatenate([lines[k] for k in range(chunk)], axis=1)
        owner = me_ref[0] ^ relative
        shapes = shapes_ref[pl.ds(pl.multiple_of(owner * modes, 8), modes), :]
        force = force + lax.dot_general(
            flat,
            shapes,
            (((1,), (1,)), ((), ())),
            precision=lax.Precision.HIGHEST,
            preferred_element_type=F32,
        )
    tile = jnp.concatenate([force, jnp.zeros((parts, LANES - modes), F32)], axis=1)
    next_keep_ref[half] = tile
    next_send_ref[half] = tile


def fold_kernel(keep_ref, got_ref, *next_refs):
    total = keep_ref[...] + got_ref[...]
    tiles = total.shape[0] - 1
    if len(next_refs) == 1:
        next_refs[0][...] = total
    else:
        half = tiles // 2
        next_refs[0][:half] = total[:half]
        next_refs[0][half] = total[tiles]
        next_refs[1][...] = total[half:]


def finish_kernel(me_ref, total_ref, panel_ref, gaf_ref, turned_ref):
    rows, chunk, parts, lanes = total_ref.shape
    chunk = chunk - 1
    force = total_ref[0, chunk]
    for i in range(rows):
        for k in range(chunk):
            at = (i * chunk + k) * lanes
            panel_ref[:, at : at + lanes] = total_ref[i, k]
        if i:
            force = force + total_ref[i, chunk]
    turned_ref[...] = jnp.transpose(force)
    share = gaf_ref.shape[0]
    gaf_ref[...] = turned_ref[pl.ds(me_ref[0] * share, share), :]


def local_call(kernel, shapes, name, *args, scratch=(), scalars=0):
    return pl.pallas_call(
        kernel,
        out_shape=tuple(jax.ShapeDtypeStruct(shape, F32) for shape in shapes),
        in_specs=[smem()] * scalars + [vmem()] * (len(args) - scalars),
        out_specs=tuple(vmem() for _ in shapes),
        scratch_shapes=list(scratch),
        compiler_params=pltpu.CompilerParams(vmem_limit_bytes=VMEM_LIMIT),
        name=name,
    )(*args)


def reversed_bits(value, count):
    out = jnp.zeros_like(value)
    bit = 1
    while bit < count:
        out = out * 2 + (value // bit) % 2
        bit *= 2
    return out


def places(owner, panel, panel_tiles):
    nx = lax.axis_size("gx")
    ny = lax.axis_size("gy")
    chunk = panel_tiles // nx
    to_x = (panel // chunk) ^ lax.axis_index("gx")
    to_y = owner ^ lax.axis_index("gy")
    return (reversed_bits(to_x, nx) * ny + reversed_bits(to_y, ny)) * chunk + panel % chunk


def swap(send, axis, bit):
    return lax.ppermute(send, axis, [(i, i ^ bit) for i in range(lax.axis_size(axis))])


def bits_of(axis):
    return [1 << b for b in range(lax.axis_size(axis).bit_length() - 1)]


def reduce_chain(keep, send, shapes, me):
    gx_bits = bits_of("gx")
    for bit in gx_bits[:-1]:
        got = swap(send, "gx", bit)
        half = keep.shape[0] // 2
        send = keep[half:] + got[half:]
        keep = keep[:half] + got[:half]
    got = swap(send, "gx", gx_bits[-1])
    owners = lax.axis_size("gy")
    order = [sum(((r >> b) & 1) * (owners >> (b + 1)) for b in range(len(bits_of("gy")))) for r in range(owners)]
    half, parts, lanes = keep.shape[0] // 2, keep.shape[1], keep.shape[2]
    shape = (half + 1, parts, lanes)
    keep, send = local_call(
        functools.partial(combine_kernel, order), (shape, shape), "combine", me, keep, got, shapes, scalars=1
    )
    for bit in bits_of("gy"):
        got = swap(send, "gy", bit)
        tiles = keep.shape[0] - 1
        if bit * 2 == owners:
            outs = (keep.shape,)
        else:
            outs = ((tiles // 2 + 1, parts, lanes),) * 2
        keep, send = (local_call(fold_kernel, outs, "fold", keep, got) + (None,))[:2]
    return keep


def body(
    state,
    right_side,
    sigma,
    coupling,
    omega,
    pressure_coef,
    tile_cells,
    tile_owner,
    tile_panel,
    interp,
    correction,
    mode_shape,
):
    modes = omega.shape[0]
    parts = 2 * modes
    panel_tiles = correction.shape[0] // LANES
    me = lax.axis_index("gy").astype(jnp.int32)[None]
    quarter = mode_shape.shape[1] // lax.axis_size("gx")
    weighted = lax.dynamic_slice_in_dim(
        mode_shape * correction[None, :], lax.axis_index("gx") * quarter, quarter, 1
    )
    shapes = lax.all_gather(weighted, "gy", axis=0, tiled=True)
    place = places(tile_owner[:, 0], tile_panel[:, 0], panel_tiles)
    halo = exchange(pack(state, modes))
    field, *edges = sweep(False, coupling, omega, pressure_coef, state, right_side, sigma, halo)
    halo = exchange(edges)
    field, table = sweep(True, coupling, omega, pressure_coef, field, right_side, sigma, halo)
    keep, send = tile_sums(place, table, tile_cells, interp, panel_tiles * lax.axis_size("gy"), parts)
    chunk = reduce_chain(keep, send, shapes, me)
    total = lax.all_gather(chunk, "gx", axis=0, tiled=False)
    share = mode_shape.shape[0] // lax.axis_size("gy")
    panels, gaf = local_call(
        finish_kernel,
        ((parts, correction.shape[0]), (share, parts)),
        "finish",
        me,
        total,
        scratch=(pltpu.VMEM((LANES, parts), F32),),
        scalars=1,
    )
    return (field, panels, gaf)


def solution(mesh):
    placed = (
        P(None, "gx", "gy"),
        P(None, "gx", "gy"),
        P("gx", "gy"),
        P(),
        P(),
        P(),
        P(("gx", "gy"), None),
        P(("gx", "gy"), None),
        P(("gx", "gy"), None),
        P(("gx", "gy"), None, None),
        P("gy"),
        P(None, "gy"),
    )
    return jax.shard_map(
        body,
        mesh=mesh,
        in_specs=placed,
        out_specs=(P(None, "gx", "gy"), P(None, "gy"), P("gy", None)),
        check_vma=False,
    )
```

```python
import functools

import jax
import jax.numpy as jnp
from jax import lax
from jax.experimental import pallas as pl
from jax.experimental.pallas import tpu as pltpu
from jax.sharding import PartitionSpec as P

F32 = jnp.float32
BF16 = jnp.bfloat16
LANES = 128
BLOCK_TILES = 32
LANE_TILES = 10
VMEM_LIMIT = 40 << 20
VMEM_ALL = 60 << 20
VMEM_SMALL = 12 << 20


def vmem():
    return pl.BlockSpec(memory_space=pltpu.VMEM)


def smem():
    return pl.BlockSpec(memory_space=pltpu.SMEM)


def pack_edges(field_ref, first, planes, row1_ref, row2_ref, col1_ref, col2_ref):
    rows, cols = field_ref.shape[1:]
    even_x = lax.rem(lax.axis_index("gx"), 2) == 0
    even_y = lax.rem(lax.axis_index("gy"), 2) == 0
    lane = lax.broadcasted_iota(jnp.int32, (rows, LANES), 1)
    left = jnp.where(even_y, col2_ref[...], col1_ref[...])
    right = jnp.where(even_y, col1_ref[...], col2_ref[...])
    for k in range(planes):
        row1_ref[0, k : k + 1, :] = field_ref[k, 0:1, :]
        row2_ref[0, k : k + 1, :] = field_ref[k, rows - 1 : rows, :]
        here = lane == first + k
        left = jnp.where(here, field_ref[k, :, 0:1], left)
        right = jnp.where(here, field_ref[k, :, cols - 1 : cols], right)
    col1_ref[...] = jnp.where(even_y, right, left)
    col2_ref[...] = jnp.where(even_y, left, right)
    up = row1_ref[0]
    down = row2_ref[0]
    row1_ref[0] = jnp.where(even_x, down, up)
    row2_ref[0] = jnp.where(even_x, up, down)


def weigh_kernel(mine_ref, shape_ref, correction_ref, weighted_ref):
    weighted_ref[...] = shape_ref[...] * correction_ref[...]


def pack_kernel(state_ref, up_ref, down_ref, left_ref, right_ref):
    mode = pl.program_id(0)
    planes = state_ref.shape[0]

    @pl.when(mode == 0)
    def _():
        left_ref[...] = jnp.zeros_like(left_ref)
        right_ref[...] = jnp.zeros_like(right_ref)

    pack_edges(state_ref, mode * planes, planes, up_ref, down_ref, left_ref, right_ref)


def sweep_kernel(
    last,
    coupling_ref,
    omega_ref,
    coef_ref,
    state_ref,
    rhs_ref,
    sigma_ref,
    row1_ref,
    row2_ref,
    col1_ref,
    col2_ref,
    new_ref,
    *rest,
):
    nbs_ref, a_ref, b_ref = rest[-3:]
    if last:
        table_ref, press_ref = rest[:2]
    mode = pl.program_id(0)
    planes, rows, cols = state_ref.shape
    nvar = planes // 2
    parts = 2 * omega_ref.shape[0]
    freq = omega_ref[mode]
    dval = 4.0 + sigma_ref[...]
    scale = 0.8 / (dval * dval + freq * freq)
    a_ref[...] = dval * scale
    b_ref[...] = freq * scale

    even_x = lax.rem(lax.axis_index("gx"), 2) == 0
    even_y = lax.rem(lax.axis_index("gy"), 2) == 0
    above_rows = jnp.where(even_x, row2_ref[0], row1_ref[0])
    below_rows = jnp.where(even_x, row1_ref[0], row2_ref[0])
    west_cols = jnp.where(even_y, col2_ref[...], col1_ref[...])
    east_cols = jnp.where(even_y, col1_ref[...], col2_ref[...])
    row = lax.broadcasted_iota(jnp.int32, (rows, cols), 0)
    lane = lax.broadcasted_iota(jnp.int32, (rows, LANES), 1)
    for k in range(planes):
        comp = mode * planes + k
        plane = state_ref[k]
        total = jnp.where(row == 0, above_rows[k : k + 1], pltpu.roll(plane, 1, 0))
        total = total + jnp.where(
            row == rows - 1, below_rows[k : k + 1], pltpu.roll(plane, rows - 1, 0)
        )
        west = pltpu.roll(west_cols, lax.rem(LANES - comp, LANES), 1)
        east = pltpu.roll(east_cols, LANES - 1 - comp, 1)
        from_west = pltpu.roll(plane, 1, 1)
        from_east = pltpu.roll(plane, cols - 1, 1)
        nbs_ref[k, :, :LANES] = (
            total[:, :LANES]
            + jnp.where(lane == 0, west, from_west[:, :LANES])
            + from_east[:, :LANES]
        )
        nbs_ref[k, :, cols - LANES :] = (
            total[:, cols - LANES :]
            + from_west[:, cols - LANES :]
            + jnp.where(lane == LANES - 1, east, from_east[:, cols - LANES :])
        )

    weight = [[coupling_ref[v, w] for w in range(nvar)] for v in range(nvar)]
    coef = [coef_ref[v] for v in range(nvar)]

    def strip(step, carry):
        here = pl.ds(pl.multiple_of(step * 8, 8), 8)
        nbs = [nbs_ref[k, here, :] for k in range(planes)]
        a = a_ref[here, :]
        b = b_ref[here, :]
        press_re = press_im = None
        for v in range(nvar):
            res_re = rhs_ref[v, here, :]
            res_im = rhs_ref[nvar + v, here, :]
            for w in range(nvar):
                res_re = res_re + weight[v][w] * nbs[w]
                res_im = res_im + weight[v][w] * nbs[nvar + w]
            new_re = 0.2 * state_ref[v, here, :] + a * res_re + b * res_im
            new_im = 0.2 * state_ref[nvar + v, here, :] + a * res_im - b * res_re
            new_ref[v, here, :] = new_re
            new_ref[nvar + v, here, :] = new_im
            if last:
                press_re = coef[v] * new_re if v == 0 else press_re + coef[v] * new_re
                press_im = coef[v] * new_im if v == 0 else press_im + coef[v] * new_im
        if last:
            for part, value in enumerate((press_re, press_im)):
                start = step * (8 * parts) + 2 * mode + part
                for half in range(cols // LANES):
                    piece = value[:, half * LANES : (half + 1) * LANES]
                    press_ref[half, pl.ds(start, 8, stride=parts), :] = piece
        return carry

    lax.fori_loop(0, rows // 8, strip, 0)
    if last:

        @pl.when(mode == pl.num_programs(0) - 1)
        def _():
            size = table_ref.shape[0] // 2
            for half in range(cols // LANES):
                whole = press_ref[half]
                high = whole.astype(BF16)
                span = slice(half * LANES, (half + 1) * LANES)
                table_ref[:size, span] = high
                table_ref[size:, span] = (whole - high.astype(F32)).astype(BF16)

    else:
        up_ref, down_ref, left_ref, right_ref = rest[:4]

        @pl.when(mode == 0)
        def _():
            left_ref[...] = jnp.zeros_like(left_ref)
            right_ref[...] = jnp.zeros_like(right_ref)

        pack_edges(new_ref, mode * planes, planes, up_ref, down_ref, left_ref, right_ref)


def edge_shapes(modes, planes, rows, cols):
    shapes = (
        jax.ShapeDtypeStruct((modes, planes, cols), F32),
        jax.ShapeDtypeStruct((modes, planes, cols), F32),
        jax.ShapeDtypeStruct((rows, LANES), F32),
        jax.ShapeDtypeStruct((rows, LANES), F32),
    )
    row_spec = pl.BlockSpec((1, planes, cols), lambda m: (m, 0, 0))
    col_spec = pl.BlockSpec((rows, LANES), lambda m: (0, 0))
    return shapes, (row_spec, row_spec, col_spec, col_spec)


def weigh(mode_shape, correction):
    count, panels = mode_shape.shape
    share = panels // lax.axis_size("gx")
    mine = lax.axis_index("gx").astype(jnp.int32)[None]
    return pl.pallas_call(
        weigh_kernel,
        grid_spec=pltpu.PrefetchScalarGridSpec(
            num_scalar_prefetch=1,
            grid=(1,),
            in_specs=[
                pl.BlockSpec((count, share), lambda g, at: (0, at[0])),
                pl.BlockSpec((1, share), lambda g, at: (0, at[0])),
            ],
            out_specs=pl.BlockSpec((count, share), lambda g, at: (0, 0)),
        ),
        out_shape=jax.ShapeDtypeStruct((count, share), F32),
        compiler_params=pltpu.CompilerParams(vmem_limit_bytes=VMEM_ALL),
        name="weigh",
    )(mine, mode_shape, correction[None, :])


def pack(state, modes):
    comp, rows, cols = state.shape
    planes = comp // modes
    shapes, specs = edge_shapes(modes, planes, rows, cols)
    return pl.pallas_call(
        pack_kernel,
        grid=(modes,),
        out_shape=shapes,
        in_specs=[pl.BlockSpec((planes, rows, cols), lambda m: (m, 0, 0))],
        out_specs=specs,
        compiler_params=pltpu.CompilerParams(vmem_limit_bytes=VMEM_LIMIT),
        name="pack",
    )(state)


def exchange(edges):
    got = []
    for axis, first, second in (("gx", edges[0], edges[1]), ("gy", edges[2], edges[3])):
        count = lax.axis_size(axis)
        got.append(swap(first, axis, 1))
        pairs = [(i, i + 1) for i in range(1, count - 1, 2)]
        got.append(lax.ppermute(second, axis, pairs + [(b, a) for a, b in pairs]))
    return got


def sweep(last, coupling, omega, coef, field, rhs, sigma, halo):
    comp, rows, cols = field.shape
    modes = omega.shape[0]
    planes = comp // modes
    edges, edge_specs = edge_shapes(modes, planes, rows, cols)
    block = pl.BlockSpec((planes, rows, cols), lambda m: (m, 0, 0))
    if last:
        table = (4 * modes * rows, cols)
        press = (cols // LANES, 2 * modes * rows, LANES)
        extra = (jax.ShapeDtypeStruct(table, BF16), jax.ShapeDtypeStruct(press, F32))
        extra_specs = (pl.BlockSpec(table, lambda m: (0, 0)), pl.BlockSpec(press, lambda m: (0, 0, 0)))
    else:
        extra, extra_specs = edges, edge_specs
    return pl.pallas_call(
        functools.partial(sweep_kernel, last),
        grid=(modes,),
        out_shape=(jax.ShapeDtypeStruct(field.shape, F32),) + extra,
        in_specs=[
            smem(),
            smem(),
            smem(),
            block,
            block,
            pl.BlockSpec((rows, cols), lambda m: (0, 0)),
            *edge_specs,
        ],
        out_specs=(block,) + extra_specs,
        scratch_shapes=[
            pltpu.VMEM((planes, rows, cols), F32),
            pltpu.VMEM((rows, cols), F32),
            pltpu.VMEM((rows, cols), F32),
        ],
        compiler_params=pltpu.CompilerParams(vmem_limit_bytes=VMEM_LIMIT),
        cost_estimate=pl.CostEstimate(flops=8 * 10**9, bytes_accessed=12 * field.size, transcendentals=0),
        name="sweep",
    )(coupling, omega, coef, field, rhs, sigma, *halo)


def tile_kernel(place_ref, table_ref, press_ref, cells_ref, interp_ref, keep_ref, send_ref, acc_ref):
    step = pl.program_id(0)
    block = cells_ref.shape[0]
    parts = acc_ref.shape[1]
    size = table_ref.shape[0] // 2
    cols = table_ref.shape[1]
    rows = size // parts
    shift = cols.bit_length() - 1

    @pl.when(step == 0)
    def _():
        acc_ref[...] = jnp.zeros_like(acc_ref)

    col_at = lax.broadcasted_iota(jnp.int16, (cols, 2 * LANES), 0)
    one = jnp.ones((), BF16)
    zero = jnp.zeros((), BF16)
    blank = jnp.zeros((2 * parts, LANES), F32)

    def by_matmul(pair):
        cells = jnp.concatenate(
            [cells_ref[2 * pair : 2 * pair + 1, :], cells_ref[2 * pair + 1 : 2 * pair + 2, :]], axis=1
        )
        col = jnp.broadcast_to((cells & (cols - 1)).astype(jnp.int16), (cols, 2 * LANES))
        hot = jnp.where(col_at == col, one, zero)
        found = jnp.dot(table_ref[...], hot, preferred_element_type=F32)
        found = (found[:size] + found[size:]).reshape(rows, parts, 2 * LANES)
        row = jnp.broadcast_to(cells >> shift, (parts, 2 * LANES))
        bit = rows // 2
        while bit:
            found = jnp.where(((row & bit) != 0)[None], found[bit:], found[:bit])
            bit //= 2
        return found[0]

    halves = cols // LANES
    lane_bits = LANES.bit_length() - 1

    def by_lanes(tile):
        cells = jnp.broadcast_to(cells_ref[tile : tile + 1, :], (parts, LANES))
        lane = cells & (LANES - 1)
        chosen = [(cells >> (lane_bits + b)) & 1 == 1 for b in range((rows * halves).bit_length() - 1)]

        def among(base, bits):
            if bits == 0:
                at = base // halves * parts
                return jnp.take_along_axis(press_ref[base % halves, at : at + parts, :], lane, axis=1)
            low = among(base, bits - 1)
            return jnp.where(chosen[bits - 1], among(base + (1 << (bits - 1)), bits - 1), low)

        return among(0, len(chosen))

    by_lane_count = LANE_TILES * block // BLOCK_TILES // 2 * 2
    pairs = (block - by_lane_count) // 2
    surfs = []
    beside = []
    for pair in range(pairs):
        for tile in range(pair * by_lane_count // pairs, (pair + 1) * by_lane_count // pairs):
            beside.append(by_lanes(block - by_lane_count + tile))
        surfs.append(by_matmul(pair))
    for pair in range(by_lane_count // 2):
        surfs.append(jnp.concatenate(beside[2 * pair : 2 * pair + 2], axis=1))
    for pair, surf in enumerate(surfs):
        high = surf.astype(BF16).astype(F32)
        split = jnp.concatenate([high, surf - high], axis=0)
        left = jnp.concatenate(
            [
                jnp.concatenate([split[:, :LANES], blank], axis=1),
                jnp.concatenate([blank, split[:, LANES:]], axis=1),
            ],
            axis=0,
        ).astype(BF16)
        weight = interp_ref[2 * pair : 2 * pair + 2].reshape(2 * LANES, LANES)
        weight_high = weight.astype(BF16)
        weight_low = (weight - weight_high.astype(F32)).astype(BF16)
        right = jnp.concatenate([weight_high, weight_low], axis=1)
        out = jnp.dot(left, right, preferred_element_type=F32)
        for side in range(2):
            line = out[side * 2 * parts : (side + 1) * 2 * parts]
            high_part = line[:parts, :LANES] + line[:parts, LANES:]
            at = place_ref[step * block + 2 * pair + side]
            acc_ref[at] += high_part + line[parts:, :LANES]

    @pl.when(step == pl.num_programs(0) - 1)
    def _():
        half = keep_ref.shape[0]
        keep_ref[...] = acc_ref[:half]
        send_ref[...] = acc_ref[half:]


def tile_sums(place, table, press, cells, interp, panel_tiles, parts):
    tiles = cells.shape[0]
    half = (panel_tiles // 2, parts, LANES)
    block = min(BLOCK_TILES, tiles)
    return pl.pallas_call(
        tile_kernel,
        grid=(tiles // block,),
        out_shape=(jax.ShapeDtypeStruct(half, F32), jax.ShapeDtypeStruct(half, F32)),
        in_specs=[
            smem(),
            pl.BlockSpec(table.shape, lambda i: (0, 0)),
            pl.BlockSpec(press.shape, lambda i: (0, 0, 0)),
            pl.BlockSpec((block, LANES), lambda i: (i, 0)),
            pl.BlockSpec((block, LANES, LANES), lambda i: (i, 0, 0)),
        ],
        out_specs=(pl.BlockSpec(half, lambda i: (0, 0, 0)), pl.BlockSpec(half, lambda i: (0, 0, 0))),
        scratch_shapes=[pltpu.VMEM((panel_tiles, parts, LANES), F32)],
        compiler_params=pltpu.CompilerParams(vmem_limit_bytes=VMEM_LIMIT),
        cost_estimate=pl.CostEstimate(
            flops=2 * table.size * cells.size, bytes_accessed=4 * interp.size, transcendentals=0
        ),
        name="tiles",
    )(place, table, press, cells, interp)


def combine_kernel(order, keep_ref, got_ref, shapes_ref, *out_refs):
    owners = len(order)
    chunk = keep_ref.shape[0] // owners
    parts = keep_ref.shape[1]
    modes = shapes_ref.shape[0] // owners
    tiles = out_refs[0].shape[0] - 1
    force = jnp.zeros((parts, modes), F32)
    for at, relative in enumerate(order):
        first = at * chunk
        lines = keep_ref[first : first + chunk] + got_ref[first : first + chunk]
        out_refs[first // tiles][first % tiles : first % tiles + chunk] = lines
        force = force + lax.dot_general(
            jnp.concatenate([lines[k] for k in range(chunk)], axis=1),
            shapes_ref[relative * modes : (relative + 1) * modes, :],
            (((1,), (1,)), ((), ())),
            precision=lax.Precision.HIGHEST,
            preferred_element_type=F32,
        )
    tile = jnp.concatenate([force, jnp.zeros((parts, LANES - modes), F32)], axis=1)
    for out_ref in out_refs:
        out_ref[tiles] = tile


def fold_kernel(count, *refs):
    total = refs[0][...]
    for ref in refs[1:count]:
        total = total + ref[...]
    tiles = refs[count].shape[0] - 1
    for number, ref in enumerate(refs[count:]):
        ref[:tiles] = total[number * tiles : (number + 1) * tiles]
        ref[tiles] = total[total.shape[0] - 1]


def finish_kernel(*refs):
    *total_refs, panel_ref, gaf_ref, turned_ref = refs
    chunk, parts, lanes = total_refs[0].shape
    chunk = chunk - 1
    here = lax.axis_index("gx")
    force = total_refs[0][chunk]
    for relative, total_ref in enumerate(total_refs):
        first = (here ^ relative) * (chunk * lanes)
        for k in range(chunk):
            panel_ref[:, pl.ds(pl.multiple_of(first + k * lanes, lanes), lanes)] = total_ref[k]
        if relative:
            force = force + total_ref[chunk]
    turned_ref[...] = jnp.transpose(force)
    share = gaf_ref.shape[0]
    gaf_ref[...] = turned_ref[pl.ds(lax.axis_index("gy") * share, share), :]


def local_call(kernel, shapes, name, *args, scratch=(), scalars=0):
    return pl.pallas_call(
        kernel,
        out_shape=tuple(jax.ShapeDtypeStruct(shape, F32) for shape in shapes),
        in_specs=[smem()] * scalars + [vmem()] * (len(args) - scalars),
        out_specs=tuple(vmem() for _ in shapes),
        scratch_shapes=list(scratch),
        compiler_params=pltpu.CompilerParams(vmem_limit_bytes=VMEM_SMALL),
        name=name,
    )(*args)


def reversed_bits(value, count):
    out = jnp.zeros_like(value)
    bit = 1
    while bit < count:
        out = out * 2 + (value // bit) % 2
        bit *= 2
    return out


def places(owner, panel, panel_tiles):
    nx = lax.axis_size("gx")
    ny = lax.axis_size("gy")
    chunk = panel_tiles // nx
    to_x = (panel // chunk) ^ lax.axis_index("gx")
    to_y = owner ^ lax.axis_index("gy")
    return (reversed_bits(to_x, nx) * ny + position(to_y, "gy")) * chunk + panel % chunk


def swap(send, axis, bit):
    return lax.ppermute(send, axis, [(i, i ^ bit) for i in range(lax.axis_size(axis))])


def gather_step(blocks, axis, bit):
    held = sorted(blocks)
    got = swap(jnp.concatenate([blocks[r] for r in held], axis=0), axis, bit)
    return {**blocks, **{r ^ bit: block for r, block in zip(held, jnp.split(got, len(held), axis=0))}}


def bits_of(axis):
    return [1 << b for b in range(lax.axis_size(axis).bit_length() - 1)]


def levels(axis):
    found = []
    base = 1
    while base < lax.axis_size(axis):
        size = min(4, lax.axis_size(axis) // base)
        found.append((base, size))
        base *= size
    return found


def position(relative, axis):
    at = 0
    for base, size in levels(axis):
        at = at * size + relative // base % size
    return at


def reduce_panels(keep, send, shapes):
    gx_bits = bits_of("gx")
    for bit in gx_bits[:-1]:
        got = swap(send, "gx", bit)
        half = keep.shape[0] // 2
        send = keep[half:] + got[half:]
        keep = keep[:half] + got[:half]
    got = swap(send, "gx", gx_bits[-1])
    owners = lax.axis_size("gy")
    order = sorted(range(owners), key=lambda relative: position(relative, "gy"))
    steps = levels("gy")
    tiles = keep.shape[0] // steps[0][1]
    lines = keep.shape[1:]
    held = local_call(
        functools.partial(combine_kernel, order), ((tiles + 1,) + lines,) * steps[0][1], "combine", keep, got, shapes
    )
    for number, (base, size) in enumerate(steps):
        held = [held[0]] + [swap(held[r], "gy", base * r) for r in range(1, size)]
        parts = steps[number + 1][1] if number + 1 < len(steps) else 1
        tiles = tiles // parts
        held = local_call(functools.partial(fold_kernel, size), ((tiles + 1,) + lines,) * parts, "fold", *held)
    return held[0]


def body(
    state,
    right_side,
    sigma,
    coupling,
    omega,
    pressure_coef,
    tile_cells,
    tile_owner,
    tile_panel,
    interp,
    correction,
    mode_shape,
):
    modes = omega.shape[0]
    parts = 2 * modes
    panel_tiles = correction.shape[0] // LANES
    place = places(tile_owner[:, 0], tile_panel[:, 0], panel_tiles)
    halo = exchange(pack(state, modes))
    weighted = weigh(mode_shape, correction)
    far = bits_of("gy")[::-1]
    blocks = gather_step({0: weighted}, "gy", far[0])
    field, *edges = sweep(False, coupling, omega, pressure_coef, state, right_side, sigma, halo)
    edges, blocks = lax.optimization_barrier((edges, blocks))
    halo = exchange(edges)
    for bit in far[1:-1]:
        blocks = gather_step(blocks, "gy", bit)
    field, table, press = sweep(True, coupling, omega, pressure_coef, field, right_side, sigma, halo)
    table, blocks = lax.optimization_barrier((table, blocks))
    blocks = gather_step(blocks, "gy", far[-1])
    shapes = jnp.concatenate([blocks[r] for r in sorted(blocks)], axis=0)
    keep, send = tile_sums(place, table, press, tile_cells, interp, panel_tiles * lax.axis_size("gy"), parts)
    send, shapes = lax.optimization_barrier((send, shapes))
    chunk = reduce_panels(keep, send, shapes)
    total = [chunk] + [swap(chunk, "gx", relative) for relative in range(1, lax.axis_size("gx"))]
    share = mode_shape.shape[0] // lax.axis_size("gy")
    panels, gaf = local_call(
        finish_kernel,
        ((parts, correction.shape[0]), (share, parts)),
        "finish",
        *total,
        scratch=(pltpu.VMEM((LANES, parts), F32),),
    )
    return (field, panels, gaf)


def solution(mesh):
    placed = (
        P(None, "gx", "gy"),
        P(None, "gx", "gy"),
        P("gx", "gy"),
        P(),
        P(),
        P(),
        P(("gx", "gy"), None),
        P(("gx", "gy"), None),
        P(("gx", "gy"), None),
        P(("gx", "gy"), None, None),
        P("gy"),
        P(None, "gy"),
    )
    return jax.shard_map(
        body,
        mesh=mesh,
        in_specs=placed,
        out_specs=(P(None, "gx", "gy"), P(None, "gy"), P("gy", None)),
        check_vma=False,
    )
```

```python
import functools

import jax
import jax.numpy as jnp
from jax import lax
from jax.experimental import pallas as pl
from jax.experimental.pallas import tpu as pltpu
from jax.sharding import PartitionSpec as P

F32 = jnp.float32
BF16 = jnp.bfloat16
LANES = 128
BLOCK_TILES = 32
LANE_TILES = 10
VMEM_LIMIT = 40 << 20
VMEM_ALL = 60 << 20
VMEM_SWEEP = 46 << 20
VMEM_SMALL = 12 << 20


def vmem():
    return pl.BlockSpec(memory_space=pltpu.VMEM)


def smem():
    return pl.BlockSpec(memory_space=pltpu.SMEM)


def pack_edges(field_ref, first, planes, row1_ref, row2_ref, col1_ref, col2_ref):
    rows, cols = field_ref.shape[1:]
    even_x = lax.rem(lax.axis_index("gx"), 2) == 0
    even_y = lax.rem(lax.axis_index("gy"), 2) == 0
    lane = lax.broadcasted_iota(jnp.int32, (rows, LANES), 1)
    left = jnp.where(even_y, col2_ref[...], col1_ref[...])
    right = jnp.where(even_y, col1_ref[...], col2_ref[...])
    for k in range(planes):
        row1_ref[0, k : k + 1, :] = field_ref[k, 0:1, :]
        row2_ref[0, k : k + 1, :] = field_ref[k, rows - 1 : rows, :]
        here = lane == first + k
        left = jnp.where(here, field_ref[k, :, 0:1], left)
        right = jnp.where(here, field_ref[k, :, cols - 1 : cols], right)
    col1_ref[...] = jnp.where(even_y, right, left)
    col2_ref[...] = jnp.where(even_y, left, right)
    up = row1_ref[0]
    down = row2_ref[0]
    row1_ref[0] = jnp.where(even_x, down, up)
    row2_ref[0] = jnp.where(even_x, up, down)


def pack_kernel(
    modes,
    state_ref,
    shape_ref,
    correction_ref,
    owner_ref,
    panel_ref,
    row1_ref,
    row2_ref,
    col1_ref,
    col2_ref,
    weighted_ref,
    place_ref,
    held_ref,
    shapes_ref,
    factor_ref,
    tiles_ref,
    sems,
):
    planes = state_ref.shape[0] // modes
    share = weighted_ref.shape[1]
    copies = []
    for mode in range(modes):
        block = pl.ds(mode * planes, planes)
        copies.append(pltpu.make_async_copy(state_ref.at[block], held_ref.at[block], sems.at[mode]))
    mine = pl.ds(pl.multiple_of(lax.axis_index("gx") * share, LANES), share)
    copies.append(pltpu.make_async_copy(shape_ref.at[:, mine], shapes_ref, sems.at[modes]))
    copies.append(pltpu.make_async_copy(correction_ref.at[:, mine], factor_ref, sems.at[modes + 1]))
    copies.append(pltpu.make_async_copy(owner_ref, tiles_ref.at[0], sems.at[modes + 2]))
    copies.append(pltpu.make_async_copy(panel_ref, tiles_ref.at[1], sems.at[modes + 3]))
    for copy in copies:
        copy.start()
    col1_ref[...] = jnp.zeros_like(col1_ref)
    col2_ref[...] = jnp.zeros_like(col2_ref)
    for mode in range(modes):
        copies[mode].wait()
        here = pl.ds(mode, 1)
        block = pl.ds(mode * planes, planes)
        pack_edges(
            held_ref.at[block], mode * planes, planes, row1_ref.at[here], row2_ref.at[here], col1_ref, col2_ref
        )
    for copy in copies[modes:]:
        copy.wait()
    weighted_ref[...] = shapes_ref[...] * factor_ref[...]
    place_ref[...] = places(tiles_ref[0], tiles_ref[1], shape_ref.shape[1] // LANES)


def sweep_kernel(
    last,
    coupling_ref,
    omega_ref,
    coef_ref,
    state_ref,
    right_ref,
    sigma_ref,
    row1_ref,
    row2_ref,
    col1_ref,
    col2_ref,
    new_ref,
    *rest,
):
    nbs_ref, a_ref, b_ref, rhs_ref, sems = rest[-5:]
    if last:
        table_ref, press_ref = rest[:2]
    mode = pl.program_id(0)
    planes, rows, cols = state_ref.shape
    nvar = planes // 2
    parts = 2 * omega_ref.shape[0]
    slot = lax.rem(mode, 2)

    def fetch(which):
        into = lax.rem(which, 2)
        block = pl.ds(which * planes, planes)
        return pltpu.make_async_copy(right_ref.at[block], rhs_ref.at[into], sems.at[into])

    @pl.when(mode == 0)
    def _():
        fetch(mode).start()

    @pl.when(mode + 1 < pl.num_programs(0))
    def _():
        fetch(mode + 1).start()

    freq = omega_ref[mode]
    dval = 4.0 + sigma_ref[...]
    scale = 0.8 / (dval * dval + freq * freq)
    a_ref[...] = dval * scale
    b_ref[...] = freq * scale

    even_x = lax.rem(lax.axis_index("gx"), 2) == 0
    even_y = lax.rem(lax.axis_index("gy"), 2) == 0
    above_rows = jnp.where(even_x, row2_ref[0], row1_ref[0])
    below_rows = jnp.where(even_x, row1_ref[0], row2_ref[0])
    west_cols = jnp.where(even_y, col2_ref[...], col1_ref[...])
    east_cols = jnp.where(even_y, col1_ref[...], col2_ref[...])
    row = lax.broadcasted_iota(jnp.int32, (rows, cols), 0)
    lane = lax.broadcasted_iota(jnp.int32, (rows, LANES), 1)
    for k in range(planes):
        comp = mode * planes + k
        plane = state_ref[k]
        total = jnp.where(row == 0, above_rows[k : k + 1], pltpu.roll(plane, 1, 0))
        total = total + jnp.where(
            row == rows - 1, below_rows[k : k + 1], pltpu.roll(plane, rows - 1, 0)
        )
        west = pltpu.roll(west_cols, lax.rem(LANES - comp, LANES), 1)
        east = pltpu.roll(east_cols, LANES - 1 - comp, 1)
        from_west = pltpu.roll(plane, 1, 1)
        from_east = pltpu.roll(plane, cols - 1, 1)
        nbs_ref[k, :, :LANES] = (
            total[:, :LANES]
            + jnp.where(lane == 0, west, from_west[:, :LANES])
            + from_east[:, :LANES]
        )
        nbs_ref[k, :, cols - LANES :] = (
            total[:, cols - LANES :]
            + from_west[:, cols - LANES :]
            + jnp.where(lane == LANES - 1, east, from_east[:, cols - LANES :])
        )

    weight = [[coupling_ref[v, w] for w in range(nvar)] for v in range(nvar)]
    coef = [coef_ref[v] for v in range(nvar)]

    def strip(step, carry):
        here = pl.ds(pl.multiple_of(step * 8, 8), 8)
        nbs = [nbs_ref[k, here, :] for k in range(planes)]
        a = a_ref[here, :]
        b = b_ref[here, :]
        press_re = press_im = None
        for v in range(nvar):
            res_re = rhs_ref[slot, v, here, :]
            res_im = rhs_ref[slot, nvar + v, here, :]
            for w in range(nvar):
                res_re = res_re + weight[v][w] * nbs[w]
                res_im = res_im + weight[v][w] * nbs[nvar + w]
            new_re = 0.2 * state_ref[v, here, :] + a * res_re + b * res_im
            new_im = 0.2 * state_ref[nvar + v, here, :] + a * res_im - b * res_re
            new_ref[v, here, :] = new_re
            new_ref[nvar + v, here, :] = new_im
            if last:
                press_re = coef[v] * new_re if v == 0 else press_re + coef[v] * new_re
                press_im = coef[v] * new_im if v == 0 else press_im + coef[v] * new_im
        if last:
            for part, value in enumerate((press_re, press_im)):
                start = step * (8 * parts) + 2 * mode + part
                for half in range(cols // LANES):
                    piece = value[:, half * LANES : (half + 1) * LANES]
                    press_ref[half, pl.ds(start, 8, stride=parts), :] = piece
        return carry

    fetch(mode).wait()
    lax.fori_loop(0, rows // 8, strip, 0, unroll=True)
    if last:

        @pl.when(mode == pl.num_programs(0) - 1)
        def _():
            size = table_ref.shape[0] // 2
            for half in range(cols // LANES):
                whole = press_ref[half]
                high = whole.astype(BF16)
                span = slice(half * LANES, (half + 1) * LANES)
                table_ref[:size, span] = high
                table_ref[size:, span] = (whole - high.astype(F32)).astype(BF16)

    else:
        up_ref, down_ref, left_ref, right_ref = rest[:4]

        @pl.when(mode == 0)
        def _():
            left_ref[...] = jnp.zeros_like(left_ref)
            right_ref[...] = jnp.zeros_like(right_ref)

        pack_edges(new_ref, mode * planes, planes, up_ref, down_ref, left_ref, right_ref)


def edge_shapes(modes, planes, rows, cols):
    shapes = (
        jax.ShapeDtypeStruct((modes, planes, cols), F32),
        jax.ShapeDtypeStruct((modes, planes, cols), F32),
        jax.ShapeDtypeStruct((rows, LANES), F32),
        jax.ShapeDtypeStruct((rows, LANES), F32),
    )
    row_spec = pl.BlockSpec((1, planes, cols), lambda m: (m, 0, 0))
    col_spec = pl.BlockSpec((rows, LANES), lambda m: (0, 0))
    return shapes, (row_spec, row_spec, col_spec, col_spec)


def pack(state, modes, mode_shape, correction, owner, panel):
    comp, rows, cols = state.shape
    shapes, _ = edge_shapes(modes, comp // modes, rows, cols)
    share = (mode_shape.shape[0], mode_shape.shape[1] // lax.axis_size("gx"))
    hbm = pl.BlockSpec(memory_space=pltpu.HBM)
    return pl.pallas_call(
        functools.partial(pack_kernel, modes),
        out_shape=shapes + (jax.ShapeDtypeStruct(share, F32), jax.ShapeDtypeStruct(owner.shape, jnp.int32)),
        in_specs=[hbm] * 5,
        out_specs=(vmem(),) * 6,
        scratch_shapes=[
            pltpu.VMEM(state.shape, F32),
            pltpu.VMEM(share, F32),
            pltpu.VMEM((1, share[1]), F32),
            pltpu.VMEM((2,) + owner.shape, jnp.int32),
            pltpu.SemaphoreType.DMA((modes + 4,)),
        ],
        compiler_params=pltpu.CompilerParams(vmem_limit_bytes=VMEM_ALL),
        name="pack",
    )(state, mode_shape, correction[None, :], owner, panel)


def exchange(edges):
    got = []
    for axis, first, second in (("gx", edges[0], edges[1]), ("gy", edges[2], edges[3])):
        count = lax.axis_size(axis)
        got.append(swap(first, axis, 1))
        pairs = [(i, i + 1) for i in range(1, count - 1, 2)]
        got.append(lax.ppermute(second, axis, pairs + [(b, a) for a, b in pairs]))
    return got


def sweep(last, coupling, omega, coef, field, rhs, sigma, halo):
    comp, rows, cols = field.shape
    modes = omega.shape[0]
    planes = comp // modes
    edges, edge_specs = edge_shapes(modes, planes, rows, cols)
    block = pl.BlockSpec((planes, rows, cols), lambda m: (m, 0, 0))
    if last:
        table = (4 * modes * rows, cols)
        press = (cols // LANES, 2 * modes * rows, LANES)
        extra = (jax.ShapeDtypeStruct(table, BF16), jax.ShapeDtypeStruct(press, F32))
        extra_specs = (pl.BlockSpec(table, lambda m: (0, 0)), pl.BlockSpec(press, lambda m: (0, 0, 0)))
    else:
        extra, extra_specs = edges, edge_specs
    return pl.pallas_call(
        functools.partial(sweep_kernel, last),
        grid=(modes,),
        out_shape=(jax.ShapeDtypeStruct(field.shape, F32),) + extra,
        in_specs=[
            smem(),
            smem(),
            smem(),
            block,
            pl.BlockSpec(memory_space=pltpu.HBM),
            pl.BlockSpec((rows, cols), lambda m: (0, 0)),
            *edge_specs,
        ],
        out_specs=(block,) + extra_specs,
        scratch_shapes=[
            pltpu.VMEM((planes, rows, cols), F32),
            pltpu.VMEM((rows, cols), F32),
            pltpu.VMEM((rows, cols), F32),
            pltpu.VMEM((2, planes, rows, cols), F32),
            pltpu.SemaphoreType.DMA((2,)),
        ],
        compiler_params=pltpu.CompilerParams(vmem_limit_bytes=VMEM_SWEEP),
        cost_estimate=pl.CostEstimate(flops=8 * 10**9, bytes_accessed=12 * field.size, transcendentals=0),
        name="sweep",
    )(coupling, omega, coef, field, rhs, sigma, *halo)


def tile_kernel(place_ref, table_ref, press_ref, cells_ref, interp_ref, keep_ref, send_ref, acc_ref):
    step = pl.program_id(0)
    block = cells_ref.shape[0]
    parts = acc_ref.shape[1]
    size = table_ref.shape[0] // 2
    cols = table_ref.shape[1]
    rows = size // parts
    shift = cols.bit_length() - 1

    @pl.when(step == 0)
    def _():
        acc_ref[...] = jnp.zeros_like(acc_ref)

    col_at = lax.broadcasted_iota(jnp.int16, (cols, 2 * LANES), 0)
    one = jnp.ones((), BF16)
    zero = jnp.zeros((), BF16)
    blank = jnp.zeros((2 * parts, LANES), F32)

    def by_matmul(pair):
        cells = jnp.concatenate(
            [cells_ref[2 * pair : 2 * pair + 1, :], cells_ref[2 * pair + 1 : 2 * pair + 2, :]], axis=1
        )
        col = jnp.broadcast_to((cells & (cols - 1)).astype(jnp.int16), (cols, 2 * LANES))
        hot = jnp.where(col_at == col, one, zero)
        found = jnp.dot(table_ref[...], hot, preferred_element_type=F32)
        found = (found[:size] + found[size:]).reshape(rows, parts, 2 * LANES)
        row = jnp.broadcast_to(cells >> shift, (parts, 2 * LANES))
        bit = rows // 2
        while bit:
            found = jnp.where(((row & bit) != 0)[None], found[bit:], found[:bit])
            bit //= 2
        return found[0]

    halves = cols // LANES
    lane_bits = LANES.bit_length() - 1

    def by_lanes(tile):
        cells = jnp.broadcast_to(cells_ref[tile : tile + 1, :], (parts, LANES))
        lane = cells & (LANES - 1)
        chosen = [(cells >> (lane_bits + b)) & 1 == 1 for b in range((rows * halves).bit_length() - 1)]

        def among(base, bits):
            if bits == 0:
                at = base // halves * parts
                return jnp.take_along_axis(press_ref[base % halves, at : at + parts, :], lane, axis=1)
            low = among(base, bits - 1)
            return jnp.where(chosen[bits - 1], among(base + (1 << (bits - 1)), bits - 1), low)

        return among(0, len(chosen))

    by_lane_count = LANE_TILES * block // BLOCK_TILES // 2 * 2
    pairs = (block - by_lane_count) // 2
    surfs = []
    beside = []
    for pair in range(pairs):
        for tile in range(pair * by_lane_count // pairs, (pair + 1) * by_lane_count // pairs):
            beside.append(by_lanes(block - by_lane_count + tile))
        surfs.append(by_matmul(pair))
    for pair in range(by_lane_count // 2):
        surfs.append(jnp.concatenate(beside[2 * pair : 2 * pair + 2], axis=1))
    for pair, surf in enumerate(surfs):
        high = surf.astype(BF16).astype(F32)
        split = jnp.concatenate([high, surf - high], axis=0)
        left = jnp.concatenate(
            [
                jnp.concatenate([split[:, :LANES], blank], axis=1),
                jnp.concatenate([blank, split[:, LANES:]], axis=1),
            ],
            axis=0,
        ).astype(BF16)
        weight = interp_ref[2 * pair : 2 * pair + 2].reshape(2 * LANES, LANES)
        weight_high = weight.astype(BF16)
        weight_low = (weight - weight_high.astype(F32)).astype(BF16)
        right = jnp.concatenate([weight_high, weight_low], axis=1)
        out = jnp.dot(left, right, preferred_element_type=F32)
        for side in range(2):
            line = out[side * 2 * parts : (side + 1) * 2 * parts]
            high_part = line[:parts, :LANES] + line[:parts, LANES:]
            at = place_ref[step * block + 2 * pair + side]
            acc_ref[at] += high_part + line[parts:, :LANES]

    @pl.when(step == pl.num_programs(0) - 1)
    def _():
        half = keep_ref.shape[0]
        keep_ref[...] = acc_ref[:half]
        send_ref[...] = acc_ref[half:]


def tile_sums(place, table, press, cells, interp, panel_tiles, parts):
    tiles = cells.shape[0]
    half = (panel_tiles // 2, parts, LANES)
    block = min(BLOCK_TILES, tiles)
    return pl.pallas_call(
        tile_kernel,
        grid=(tiles // block,),
        out_shape=(jax.ShapeDtypeStruct(half, F32), jax.ShapeDtypeStruct(half, F32)),
        in_specs=[
            smem(),
            pl.BlockSpec(table.shape, lambda i: (0, 0)),
            pl.BlockSpec(press.shape, lambda i: (0, 0, 0)),
            pl.BlockSpec((block, LANES), lambda i: (i, 0)),
            pl.BlockSpec((block, LANES, LANES), lambda i: (i, 0, 0)),
        ],
        out_specs=(pl.BlockSpec(half, lambda i: (0, 0, 0)), pl.BlockSpec(half, lambda i: (0, 0, 0))),
        scratch_shapes=[pltpu.VMEM((panel_tiles, parts, LANES), F32)],
        compiler_params=pltpu.CompilerParams(vmem_limit_bytes=VMEM_LIMIT),
        cost_estimate=pl.CostEstimate(
            flops=2 * table.size * cells.size, bytes_accessed=4 * interp.size, transcendentals=0
        ),
        name="tiles",
    )(place, table, press, cells, interp)


def combine_kernel(order, where, keep_ref, got_ref, *refs):
    owners = len(order)
    chunk = keep_ref.shape[0] // owners
    parts = keep_ref.shape[1]
    pieces = 1 + max(piece for piece, _ in where.values())
    shape_refs, out_refs = refs[:pieces], refs[pieces:]
    modes = shape_refs[0].shape[0]
    tiles = out_refs[0].shape[0] - 1
    force = jnp.zeros((parts, modes), F32)
    for at, relative in enumerate(order):
        first = at * chunk
        lines = keep_ref[first : first + chunk] + got_ref[first : first + chunk]
        out_refs[first // tiles][first % tiles : first % tiles + chunk] = lines
        force = force + lax.dot_general(
            jnp.concatenate([lines[k] for k in range(chunk)], axis=1),
            shape_refs[where[relative][0]][where[relative][1] : where[relative][1] + modes, :],
            (((1,), (1,)), ((), ())),
            precision=lax.Precision.HIGHEST,
            preferred_element_type=F32,
        )
    tile = jnp.concatenate([force, jnp.zeros((parts, LANES - modes), F32)], axis=1)
    for out_ref in out_refs:
        out_ref[tiles] = tile


def fold_kernel(count, *refs):
    total = refs[0][...]
    for ref in refs[1:count]:
        total = total + ref[...]
    tiles = refs[count].shape[0] - 1
    for number, ref in enumerate(refs[count:]):
        ref[:tiles] = total[number * tiles : (number + 1) * tiles]
        ref[tiles] = total[total.shape[0] - 1]


def finish_kernel(*refs):
    *total_refs, panel_ref, gaf_ref, turned_ref = refs
    chunk, parts, lanes = total_refs[0].shape
    chunk = chunk - 1
    here = lax.axis_index("gx")
    force = total_refs[0][chunk]
    for relative, total_ref in enumerate(total_refs):
        first = (here ^ relative) * (chunk * lanes)
        for k in range(chunk):
            panel_ref[:, pl.ds(pl.multiple_of(first + k * lanes, lanes), lanes)] = total_ref[k]
        if relative:
            force = force + total_ref[chunk]
    turned_ref[...] = jnp.transpose(force)
    share = gaf_ref.shape[0]
    gaf_ref[...] = turned_ref[pl.ds(lax.axis_index("gy") * share, share), :]


def local_call(kernel, shapes, name, *args, scratch=(), scalars=0):
    return pl.pallas_call(
        kernel,
        out_shape=tuple(jax.ShapeDtypeStruct(shape, F32) for shape in shapes),
        in_specs=[smem()] * scalars + [vmem()] * (len(args) - scalars),
        out_specs=tuple(vmem() for _ in shapes),
        scratch_shapes=list(scratch),
        compiler_params=pltpu.CompilerParams(vmem_limit_bytes=VMEM_SMALL),
        name=name,
    )(*args)


def reversed_bits(value, count):
    out = jnp.zeros_like(value)
    for bit in range(count.bit_length() - 1):
        out = out * 2 + ((value >> bit) & 1)
    return out


def places(owner, panel, panel_tiles):
    nx = lax.axis_size("gx")
    ny = lax.axis_size("gy")
    chunk = panel_tiles // nx
    to_x = (panel >> (chunk.bit_length() - 1)) ^ lax.axis_index("gx")
    to_y = owner ^ lax.axis_index("gy")
    return (reversed_bits(to_x, nx) * ny + position(to_y, "gy")) * chunk + (panel & (chunk - 1))


def swap(send, axis, bit):
    return lax.ppermute(send, axis, [(i, i ^ bit) for i in range(lax.axis_size(axis))])


def gather_step(pieces, axis, bit):
    whole = pieces[0] if len(pieces) == 1 else jnp.concatenate(pieces, axis=0)
    return pieces + [swap(whole, axis, bit)]


def gathered(bits, size):
    laid = [0]
    where = {0: (0, 0)}
    for number, bit in enumerate(bits):
        for at, relative in enumerate(laid):
            where[relative ^ bit] = (number + 1, at * size)
        laid = laid + [relative ^ bit for relative in laid]
    return where


def bits_of(axis):
    return [1 << b for b in range(lax.axis_size(axis).bit_length() - 1)]


def levels(axis):
    found = []
    base = 1
    while base < lax.axis_size(axis):
        size = min(4, lax.axis_size(axis) // base)
        found.append((base, size))
        base *= size
    return found


def position(relative, axis):
    at = 0
    for base, size in levels(axis):
        at = at * size + ((relative >> (base.bit_length() - 1)) & (size - 1))
    return at


def reduce_panels(keep, send, pieces, where):
    gx_bits = bits_of("gx")
    for bit in gx_bits[:-1]:
        got = swap(send, "gx", bit)
        half = keep.shape[0] // 2
        send = keep[half:] + got[half:]
        keep = keep[:half] + got[:half]
    got = swap(send, "gx", gx_bits[-1])
    owners = lax.axis_size("gy")
    order = sorted(range(owners), key=lambda relative: position(relative, "gy"))
    steps = levels("gy")
    tiles = keep.shape[0] // steps[0][1]
    lines = keep.shape[1:]
    held = local_call(
        functools.partial(combine_kernel, order, where),
        ((tiles + 1,) + lines,) * steps[0][1],
        "combine",
        keep,
        got,
        *pieces,
    )
    for number, (base, size) in enumerate(steps):
        held = [held[0]] + [swap(held[r], "gy", base * r) for r in range(1, size)]
        parts = steps[number + 1][1] if number + 1 < len(steps) else 1
        tiles = tiles // parts
        held = local_call(functools.partial(fold_kernel, size), ((tiles + 1,) + lines,) * parts, "fold", *held)
    return held[0]


def body(
    state,
    right_side,
    sigma,
    coupling,
    omega,
    pressure_coef,
    tile_cells,
    tile_owner,
    tile_panel,
    interp,
    correction,
    mode_shape,
):
    modes = omega.shape[0]
    parts = 2 * modes
    panel_tiles = correction.shape[0] // LANES
    tiles = tile_cells.shape[0]
    owner = tile_owner.reshape(tiles // LANES, LANES)
    panel = tile_panel.reshape(tiles // LANES, LANES)
    *edges, weighted, place = pack(state, modes, mode_shape, correction, owner, panel)
    halo = exchange(edges)
    far = bits_of("gy")[::-1]
    where = gathered(far, mode_shape.shape[0])
    pieces = gather_step([weighted], "gy", far[0])
    field, *edges = sweep(False, coupling, omega, pressure_coef, state, right_side, sigma, halo)
    edges, pieces = lax.optimization_barrier((edges, pieces))
    halo = exchange(edges)
    for bit in far[1:-1]:
        pieces = gather_step(pieces, "gy", bit)
    field, table, press = sweep(True, coupling, omega, pressure_coef, field, right_side, sigma, halo)
    table, pieces = lax.optimization_barrier((table, pieces))
    pieces = gather_step(pieces, "gy", far[-1])
    keep, send = tile_sums(
        place.reshape(tiles), table, press, tile_cells, interp, panel_tiles * lax.axis_size("gy"), parts
    )
    send, pieces = lax.optimization_barrier((send, pieces))
    chunk = reduce_panels(keep, send, pieces, where)
    total = [chunk] + [swap(chunk, "gx", relative) for relative in range(1, lax.axis_size("gx"))]
    share = mode_shape.shape[0] // lax.axis_size("gy")
    panels, gaf = local_call(
        finish_kernel,
        ((parts, correction.shape[0]), (share, parts)),
        "finish",
        *total,
        scratch=(pltpu.VMEM((LANES, parts), F32),),
    )
    return (field, panels, gaf)


def solution(mesh):
    placed = (
        P(None, "gx", "gy"),
        P(None, "gx", "gy"),
        P("gx", "gy"),
        P(),
        P(),
        P(),
        P(("gx", "gy"), None),
        P(("gx", "gy"), None),
        P(("gx", "gy"), None),
        P(("gx", "gy"), None, None),
        P("gy"),
        P(None, "gy"),
    )
    return jax.shard_map(
        body,
        mesh=mesh,
        in_specs=placed,
        out_specs=(P(None, "gx", "gy"), P(None, "gy"), P("gy", None)),
        check_vma=False,
    )
```

```python
import functools

import jax
import jax.numpy as jnp
from jax import lax
from jax.experimental import pallas as pl
from jax.experimental.pallas import tpu as pltpu
from jax.sharding import PartitionSpec as P

F32 = jnp.float32
BF16 = jnp.bfloat16
LANES = 128
BLOCK_TILES = 32
LANE_TILES = 10
VMEM_LIMIT = 40 << 20
VMEM_ALL = 60 << 20
VMEM_SWEEP = 46 << 20
VMEM_SMALL = 12 << 20


def vmem():
    return pl.BlockSpec(memory_space=pltpu.VMEM)


def smem():
    return pl.BlockSpec(memory_space=pltpu.SMEM)


def pack_edges(field_ref, first, planes, row1_ref, row2_ref, col1_ref, col2_ref):
    rows, cols = field_ref.shape[1:]
    even_x = lax.rem(lax.axis_index("gx"), 2) == 0
    even_y = lax.rem(lax.axis_index("gy"), 2) == 0
    lane = lax.broadcasted_iota(jnp.int32, (rows, LANES), 1)
    left = jnp.where(even_y, col2_ref[...], col1_ref[...])
    right = jnp.where(even_y, col1_ref[...], col2_ref[...])
    for k in range(planes):
        row1_ref[0, k : k + 1, :] = field_ref[k, 0:1, :]
        row2_ref[0, k : k + 1, :] = field_ref[k, rows - 1 : rows, :]
        here = lane == first + k
        left = jnp.where(here, field_ref[k, :, 0:1], left)
        right = jnp.where(here, field_ref[k, :, cols - 1 : cols], right)
    col1_ref[...] = jnp.where(even_y, right, left)
    col2_ref[...] = jnp.where(even_y, left, right)
    up = row1_ref[0]
    down = row2_ref[0]
    row1_ref[0] = jnp.where(even_x, down, up)
    row2_ref[0] = jnp.where(even_x, up, down)


def pack_kernel(
    modes,
    state_ref,
    shape_ref,
    correction_ref,
    owner_ref,
    panel_ref,
    row1_ref,
    row2_ref,
    col1_ref,
    col2_ref,
    weighted_ref,
    place_ref,
    held_ref,
    shapes_ref,
    factor_ref,
    tiles_ref,
    sems,
):
    planes = state_ref.shape[0] // modes
    share = weighted_ref.shape[1]
    copies = []
    for mode in range(modes):
        block = pl.ds(mode * planes, planes)
        copies.append(pltpu.make_async_copy(state_ref.at[block], held_ref.at[block], sems.at[mode]))
    mine = pl.ds(pl.multiple_of(lax.axis_index("gx") * share, LANES), share)
    copies.append(pltpu.make_async_copy(shape_ref.at[:, mine], shapes_ref, sems.at[modes]))
    copies.append(pltpu.make_async_copy(correction_ref.at[:, mine], factor_ref, sems.at[modes + 1]))
    copies.append(pltpu.make_async_copy(owner_ref, tiles_ref.at[0], sems.at[modes + 2]))
    copies.append(pltpu.make_async_copy(panel_ref, tiles_ref.at[1], sems.at[modes + 3]))
    for copy in copies:
        copy.start()
    col1_ref[...] = jnp.zeros_like(col1_ref)
    col2_ref[...] = jnp.zeros_like(col2_ref)
    for mode in range(modes):
        copies[mode].wait()
        here = pl.ds(mode, 1)
        block = pl.ds(mode * planes, planes)
        pack_edges(
            held_ref.at[block], mode * planes, planes, row1_ref.at[here], row2_ref.at[here], col1_ref, col2_ref
        )
    for copy in copies[modes:]:
        copy.wait()
    weighted_ref[...] = shapes_ref[...] * factor_ref[...]
    place_ref[...] = places(tiles_ref[0], tiles_ref[1], shape_ref.shape[1] // LANES)


def sweep_kernel(
    last,
    coupling_ref,
    omega_ref,
    coef_ref,
    state_ref,
    right_ref,
    sigma_ref,
    row1_ref,
    row2_ref,
    col1_ref,
    col2_ref,
    *rest,
):
    *outs, nbs0_ref, nbs1_ref, a0_ref, a1_ref, b0_ref, b1_ref, rhs_ref, new_ref, in_sems, out_sems = rest
    nbs_refs, a_refs, b_refs = (nbs0_ref, nbs1_ref), (a0_ref, a1_ref), (b0_ref, b1_ref)
    modes = omega_ref.shape[0]
    planes, rows, cols = nbs0_ref.shape
    nvar = planes // 2
    parts = 2 * modes
    blocks = [pl.ds(mode * planes, planes) for mode in range(modes)]
    fetches = [
        pltpu.make_async_copy(right_ref.at[block], rhs_ref.at[block], in_sems.at[mode])
        for mode, block in enumerate(blocks)
    ]
    for fetch in fetches:
        fetch.start()
    if last:
        field_ref, table_ref, press_ref = outs
        sends = [
            pltpu.make_async_copy(new_ref.at[block], field_ref.at[block], out_sems.at[mode])
            for mode, block in enumerate(blocks)
        ]
    else:
        new_ref, *edge_refs = outs
        edge_refs[2][...] = jnp.zeros_like(edge_refs[2])
        edge_refs[3][...] = jnp.zeros_like(edge_refs[3])

    even_x = lax.rem(lax.axis_index("gx"), 2) == 0
    even_y = lax.rem(lax.axis_index("gy"), 2) == 0
    west_cols = jnp.where(even_y, col2_ref[...], col1_ref[...])
    east_cols = jnp.where(even_y, col1_ref[...], col2_ref[...])
    row = lax.broadcasted_iota(jnp.int32, (rows, cols), 0)
    lane = lax.broadcasted_iota(jnp.int32, (rows, LANES), 1)

    def factors(mode):
        freq = omega_ref[mode]
        dval = 4.0 + sigma_ref[...]
        scale = 0.8 / (dval * dval + freq * freq)
        a_refs[mode % 2][...] = dval * scale
        b_refs[mode % 2][...] = freq * scale

    def neighbours(mode, k):
        nbs_ref = nbs_refs[mode % 2]
        comp = mode * planes + k
        plane = state_ref[comp]
        row1 = row1_ref[mode, k : k + 1, :]
        row2 = row2_ref[mode, k : k + 1, :]
        above = jnp.where(even_x, row2, row1)
        below = jnp.where(even_x, row1, row2)
        total = jnp.where(row == 0, above, pltpu.roll(plane, 1, 0))
        total = total + jnp.where(row == rows - 1, below, pltpu.roll(plane, rows - 1, 0))
        west = pltpu.roll(west_cols, (LANES - comp) % LANES, 1)
        east = pltpu.roll(east_cols, LANES - 1 - comp, 1)
        from_west = pltpu.roll(plane, 1, 1)
        from_east = pltpu.roll(plane, cols - 1, 1)
        nbs_ref[k, :, :LANES] = (
            total[:, :LANES] + jnp.where(lane == 0, west, from_west[:, :LANES]) + from_east[:, :LANES]
        )
        nbs_ref[k, :, cols - LANES :] = (
            total[:, cols - LANES :]
            + from_west[:, cols - LANES :]
            + jnp.where(lane == LANES - 1, east, from_east[:, cols - LANES :])
        )

    weight = [[coupling_ref[v, w] for w in range(nvar)] for v in range(nvar)]
    coef = [coef_ref[v] for v in range(nvar)]

    def strip(mode, step):
        here = slice(step * 8, step * 8 + 8)
        base = mode * planes
        nbs = [nbs_refs[mode % 2][k, here, :] for k in range(planes)]
        a = a_refs[mode % 2][here, :]
        b = b_refs[mode % 2][here, :]
        press_re = press_im = None
        for v in range(nvar):
            res_re = rhs_ref[base + v, here, :]
            res_im = rhs_ref[base + nvar + v, here, :]
            for w in range(nvar):
                res_re = res_re + weight[v][w] * nbs[w]
                res_im = res_im + weight[v][w] * nbs[nvar + w]
            new_re = 0.2 * state_ref[base + v, here, :] + a * res_re + b * res_im
            new_im = 0.2 * state_ref[base + nvar + v, here, :] + a * res_im - b * res_re
            new_ref[base + v, here, :] = new_re
            new_ref[base + nvar + v, here, :] = new_im
            if last:
                press_re = coef[v] * new_re if v == 0 else press_re + coef[v] * new_re
                press_im = coef[v] * new_im if v == 0 else press_im + coef[v] * new_im
        if last:
            for part, value in enumerate((press_re, press_im)):
                start = step * (8 * parts) + 2 * mode + part
                for half in range(cols // LANES):
                    piece = value[:, half * LANES : (half + 1) * LANES]
                    press_ref[half, pl.ds(start, 8, stride=parts), :] = piece

    factors(0)
    for k in range(planes):
        neighbours(0, k)
    steps = rows // 8
    for mode in range(modes):
        fetches[mode].wait()
        if mode + 1 < modes:
            factors(mode + 1)
        for step in range(steps):
            strip(mode, step)
            if mode + 1 < modes:
                for k in range(planes * step // steps, planes * (step + 1) // steps):
                    neighbours(mode + 1, k)
        if last:
            sends[mode].start()
        else:
            here = pl.ds(mode, 1)
            pack_edges(
                new_ref.at[blocks[mode]],
                mode * planes,
                planes,
                edge_refs[0].at[here],
                edge_refs[1].at[here],
                edge_refs[2],
                edge_refs[3],
            )
    if last:
        size = table_ref.shape[0] // 2
        for half in range(cols // LANES):
            whole = press_ref[half]
            high = whole.astype(BF16)
            span = slice(half * LANES, (half + 1) * LANES)
            table_ref[:size, span] = high
            table_ref[size:, span] = (whole - high.astype(F32)).astype(BF16)
        for send in sends:
            send.wait()


def edge_shapes(modes, planes, rows, cols):
    return (
        jax.ShapeDtypeStruct((modes, planes, cols), F32),
        jax.ShapeDtypeStruct((modes, planes, cols), F32),
        jax.ShapeDtypeStruct((rows, LANES), F32),
        jax.ShapeDtypeStruct((rows, LANES), F32),
    )


def pack(state, modes, mode_shape, correction, owner, panel):
    comp, rows, cols = state.shape
    shapes = edge_shapes(modes, comp // modes, rows, cols)
    share = (mode_shape.shape[0], mode_shape.shape[1] // lax.axis_size("gx"))
    hbm = pl.BlockSpec(memory_space=pltpu.HBM)
    return pl.pallas_call(
        functools.partial(pack_kernel, modes),
        out_shape=shapes + (jax.ShapeDtypeStruct(share, F32), jax.ShapeDtypeStruct(owner.shape, jnp.int32)),
        in_specs=[hbm] * 5,
        out_specs=(vmem(),) * 6,
        scratch_shapes=[
            pltpu.VMEM(state.shape, F32),
            pltpu.VMEM(share, F32),
            pltpu.VMEM((1, share[1]), F32),
            pltpu.VMEM((2,) + owner.shape, jnp.int32),
            pltpu.SemaphoreType.DMA((modes + 4,)),
        ],
        compiler_params=pltpu.CompilerParams(vmem_limit_bytes=VMEM_ALL),
        name="pack",
    )(state, mode_shape, correction[None, :], owner, panel)


def exchange(edges):
    got = []
    for axis, first, second in (("gx", edges[0], edges[1]), ("gy", edges[2], edges[3])):
        count = lax.axis_size(axis)
        got.append(swap(first, axis, 1))
        pairs = [(i, i + 1) for i in range(1, count - 1, 2)]
        got.append(lax.ppermute(second, axis, pairs + [(b, a) for a, b in pairs]))
    return got


def sweep(last, coupling, omega, coef, field, rhs, sigma, halo):
    comp, rows, cols = field.shape
    modes = omega.shape[0]
    planes = comp // modes
    hbm = pl.BlockSpec(memory_space=pltpu.HBM)
    if last:
        extra = (
            jax.ShapeDtypeStruct((4 * modes * rows, cols), BF16),
            jax.ShapeDtypeStruct((cols // LANES, 2 * modes * rows, LANES), F32),
        )
    else:
        extra = edge_shapes(modes, planes, rows, cols)
    plane = pltpu.VMEM((rows, cols), F32)
    return pl.pallas_call(
        functools.partial(sweep_kernel, last),
        out_shape=(jax.ShapeDtypeStruct(field.shape, F32),) + extra,
        in_specs=[smem(), smem(), smem(), vmem(), hbm] + [vmem()] * 5,
        out_specs=(hbm if last else vmem(),) + (vmem(),) * len(extra),
        scratch_shapes=[
            pltpu.VMEM((planes, rows, cols), F32),
            pltpu.VMEM((planes, rows, cols), F32),
            plane,
            plane,
            plane,
            plane,
            pltpu.VMEM(rhs.shape, F32),
            pltpu.VMEM(field.shape if last else (8, LANES), F32),
            pltpu.SemaphoreType.DMA((modes,)),
            pltpu.SemaphoreType.DMA((modes,)),
        ],
        compiler_params=pltpu.CompilerParams(vmem_limit_bytes=VMEM_SWEEP),
        cost_estimate=pl.CostEstimate(flops=8 * 10**9, bytes_accessed=12 * field.size, transcendentals=0),
        name="sweep",
    )(coupling, omega, coef, field, rhs, sigma, *halo)


def tile_kernel(place_ref, table_ref, press_ref, cells_ref, interp_ref, keep_ref, send_ref, acc_ref):
    step = pl.program_id(0)
    block = cells_ref.shape[0]
    parts = acc_ref.shape[1]
    size = table_ref.shape[0] // 2
    cols = table_ref.shape[1]
    rows = size // parts
    shift = cols.bit_length() - 1

    @pl.when(step == 0)
    def _():
        acc_ref[...] = jnp.zeros_like(acc_ref)

    col_at = lax.broadcasted_iota(jnp.int16, (cols, 2 * LANES), 0)
    one = jnp.ones((), BF16)
    zero = jnp.zeros((), BF16)
    blank = jnp.zeros((2 * parts, LANES), F32)

    def by_matmul(pair):
        cells = jnp.concatenate(
            [cells_ref[2 * pair : 2 * pair + 1, :], cells_ref[2 * pair + 1 : 2 * pair + 2, :]], axis=1
        )
        col = jnp.broadcast_to((cells & (cols - 1)).astype(jnp.int16), (cols, 2 * LANES))
        hot = jnp.where(col_at == col, one, zero)
        found = jnp.dot(table_ref[...], hot, preferred_element_type=F32)
        found = (found[:size] + found[size:]).reshape(rows, parts, 2 * LANES)
        row = jnp.broadcast_to(cells >> shift, (parts, 2 * LANES))
        bit = rows // 2
        while bit:
            found = jnp.where(((row & bit) != 0)[None], found[bit:], found[:bit])
            bit //= 2
        return found[0]

    halves = cols // LANES
    lane_bits = LANES.bit_length() - 1

    def by_lanes(tile):
        cells = jnp.broadcast_to(cells_ref[tile : tile + 1, :], (parts, LANES))
        lane = cells & (LANES - 1)
        chosen = [(cells >> (lane_bits + b)) & 1 == 1 for b in range((rows * halves).bit_length() - 1)]

        def among(base, bits):
            if bits == 0:
                at = base // halves * parts
                return jnp.take_along_axis(press_ref[base % halves, at : at + parts, :], lane, axis=1)
            low = among(base, bits - 1)
            return jnp.where(chosen[bits - 1], among(base + (1 << (bits - 1)), bits - 1), low)

        return among(0, len(chosen))

    by_lane_count = LANE_TILES * block // BLOCK_TILES // 2 * 2
    pairs = (block - by_lane_count) // 2
    surfs = []
    beside = []
    for pair in range(pairs):
        for tile in range(pair * by_lane_count // pairs, (pair + 1) * by_lane_count // pairs):
            beside.append(by_lanes(block - by_lane_count + tile))
        surfs.append(by_matmul(pair))
    for pair in range(by_lane_count // 2):
        surfs.append(jnp.concatenate(beside[2 * pair : 2 * pair + 2], axis=1))
    for pair, surf in enumerate(surfs):
        high = surf.astype(BF16).astype(F32)
        split = jnp.concatenate([high, surf - high], axis=0)
        left = jnp.concatenate(
            [
                jnp.concatenate([split[:, :LANES], blank], axis=1),
                jnp.concatenate([blank, split[:, LANES:]], axis=1),
            ],
            axis=0,
        ).astype(BF16)
        weight = interp_ref[2 * pair : 2 * pair + 2].reshape(2 * LANES, LANES)
        weight_high = weight.astype(BF16)
        weight_low = (weight - weight_high.astype(F32)).astype(BF16)
        right = jnp.concatenate([weight_high, weight_low], axis=1)
        out = jnp.dot(left, right, preferred_element_type=F32)
        for side in range(2):
            line = out[side * 2 * parts : (side + 1) * 2 * parts]
            high_part = line[:parts, :LANES] + line[:parts, LANES:]
            at = place_ref[step * block + 2 * pair + side]
            acc_ref[at] += high_part + line[parts:, :LANES]

    @pl.when(step == pl.num_programs(0) - 1)
    def _():
        half = keep_ref.shape[0]
        keep_ref[...] = acc_ref[:half]
        send_ref[...] = acc_ref[half:]


def tile_sums(place, table, press, cells, interp, panel_tiles, parts):
    tiles = cells.shape[0]
    half = (panel_tiles // 2, parts, LANES)
    block = min(BLOCK_TILES, tiles)
    return pl.pallas_call(
        tile_kernel,
        grid=(tiles // block,),
        out_shape=(jax.ShapeDtypeStruct(half, F32), jax.ShapeDtypeStruct(half, F32)),
        in_specs=[
            smem(),
            pl.BlockSpec(table.shape, lambda i: (0, 0)),
            pl.BlockSpec(press.shape, lambda i: (0, 0, 0)),
            pl.BlockSpec((block, LANES), lambda i: (i, 0)),
            pl.BlockSpec((block, LANES, LANES), lambda i: (i, 0, 0)),
        ],
        out_specs=(pl.BlockSpec(half, lambda i: (0, 0, 0)), pl.BlockSpec(half, lambda i: (0, 0, 0))),
        scratch_shapes=[pltpu.VMEM((panel_tiles, parts, LANES), F32)],
        compiler_params=pltpu.CompilerParams(vmem_limit_bytes=VMEM_LIMIT),
        cost_estimate=pl.CostEstimate(
            flops=2 * table.size * cells.size, bytes_accessed=4 * interp.size, transcendentals=0
        ),
        name="tiles",
    )(place, table, press, cells, interp)


def combine_kernel(order, where, keep_ref, got_ref, *refs):
    owners = len(order)
    chunk = keep_ref.shape[0] // owners
    parts = keep_ref.shape[1]
    pieces = 1 + max(piece for piece, _ in where.values())
    shape_refs, out_refs = refs[:pieces], refs[pieces:]
    modes = shape_refs[0].shape[0]
    tiles = out_refs[0].shape[0] - 1
    force = jnp.zeros((parts, modes), F32)
    for at, relative in enumerate(order):
        first = at * chunk
        lines = keep_ref[first : first + chunk] + got_ref[first : first + chunk]
        out_refs[first // tiles][first % tiles : first % tiles + chunk] = lines
        force = force + lax.dot_general(
            jnp.concatenate([lines[k] for k in range(chunk)], axis=1),
            shape_refs[where[relative][0]][where[relative][1] : where[relative][1] + modes, :],
            (((1,), (1,)), ((), ())),
            precision=lax.Precision.HIGHEST,
            preferred_element_type=F32,
        )
    tile = jnp.concatenate([force, jnp.zeros((parts, LANES - modes), F32)], axis=1)
    for out_ref in out_refs:
        out_ref[tiles] = tile


def fold_kernel(count, *refs):
    total = refs[0][...]
    for ref in refs[1:count]:
        total = total + ref[...]
    tiles = refs[count].shape[0] - 1
    for number, ref in enumerate(refs[count:]):
        ref[:tiles] = total[number * tiles : (number + 1) * tiles]
        ref[tiles] = total[total.shape[0] - 1]


def finish_kernel(*refs):
    *total_refs, panel_ref, gaf_ref, turned_ref = refs
    chunk, parts, lanes = total_refs[0].shape
    chunk = chunk - 1
    here = lax.axis_index("gx")
    force = total_refs[0][chunk]
    for relative, total_ref in enumerate(total_refs):
        first = (here ^ relative) * (chunk * lanes)
        for k in range(chunk):
            panel_ref[:, pl.ds(pl.multiple_of(first + k * lanes, lanes), lanes)] = total_ref[k]
        if relative:
            force = force + total_ref[chunk]
    turned_ref[...] = jnp.transpose(force)
    share = gaf_ref.shape[0]
    gaf_ref[...] = turned_ref[pl.ds(lax.axis_index("gy") * share, share), :]


def local_call(kernel, shapes, name, *args, scratch=(), scalars=0):
    return pl.pallas_call(
        kernel,
        out_shape=tuple(jax.ShapeDtypeStruct(shape, F32) for shape in shapes),
        in_specs=[smem()] * scalars + [vmem()] * (len(args) - scalars),
        out_specs=tuple(vmem() for _ in shapes),
        scratch_shapes=list(scratch),
        compiler_params=pltpu.CompilerParams(vmem_limit_bytes=VMEM_SMALL),
        name=name,
    )(*args)


def reversed_bits(value, count):
    out = jnp.zeros_like(value)
    for bit in range(count.bit_length() - 1):
        out = out * 2 + ((value >> bit) & 1)
    return out


def places(owner, panel, panel_tiles):
    nx = lax.axis_size("gx")
    ny = lax.axis_size("gy")
    chunk = panel_tiles // nx
    to_x = (panel >> (chunk.bit_length() - 1)) ^ lax.axis_index("gx")
    to_y = owner ^ lax.axis_index("gy")
    return (reversed_bits(to_x, nx) * ny + position(to_y, "gy")) * chunk + (panel & (chunk - 1))


def swap(send, axis, bit):
    return lax.ppermute(send, axis, [(i, i ^ bit) for i in range(lax.axis_size(axis))])


def gather_step(pieces, axis, bit):
    whole = pieces[0] if len(pieces) == 1 else jnp.concatenate(pieces, axis=0)
    return pieces + [swap(whole, axis, bit)]


def gathered(bits, size):
    laid = [0]
    where = {0: (0, 0)}
    for number, bit in enumerate(bits):
        for at, relative in enumerate(laid):
            where[relative ^ bit] = (number + 1, at * size)
        laid = laid + [relative ^ bit for relative in laid]
    return where


def bits_of(axis):
    return [1 << b for b in range(lax.axis_size(axis).bit_length() - 1)]


def levels(axis):
    found = []
    base = 1
    while base < lax.axis_size(axis):
        size = min(4, lax.axis_size(axis) // base)
        found.append((base, size))
        base *= size
    return found


def position(relative, axis):
    at = 0
    for base, size in levels(axis):
        at = at * size + ((relative >> (base.bit_length() - 1)) & (size - 1))
    return at


def reduce_panels(keep, send, pieces, where):
    gx_bits = bits_of("gx")
    for bit in gx_bits[:-1]:
        got = swap(send, "gx", bit)
        half = keep.shape[0] // 2
        send = keep[half:] + got[half:]
        keep = keep[:half] + got[:half]
    got = swap(send, "gx", gx_bits[-1])
    owners = lax.axis_size("gy")
    order = sorted(range(owners), key=lambda relative: position(relative, "gy"))
    steps = levels("gy")
    tiles = keep.shape[0] // steps[0][1]
    lines = keep.shape[1:]
    held = local_call(
        functools.partial(combine_kernel, order, where),
        ((tiles + 1,) + lines,) * steps[0][1],
        "combine",
        keep,
        got,
        *pieces,
    )
    for number, (base, size) in enumerate(steps):
        held = [held[0]] + [swap(held[r], "gy", base * r) for r in range(1, size)]
        parts = steps[number + 1][1] if number + 1 < len(steps) else 1
        tiles = tiles // parts
        held = local_call(functools.partial(fold_kernel, size), ((tiles + 1,) + lines,) * parts, "fold", *held)
    return held[0]


def body(
    state,
    right_side,
    sigma,
    coupling,
    omega,
    pressure_coef,
    tile_cells,
    tile_owner,
    tile_panel,
    interp,
    correction,
    mode_shape,
):
    modes = omega.shape[0]
    parts = 2 * modes
    panel_tiles = correction.shape[0] // LANES
    tiles = tile_cells.shape[0]
    owner = tile_owner.reshape(tiles // LANES, LANES)
    panel = tile_panel.reshape(tiles // LANES, LANES)
    *edges, weighted, place = pack(state, modes, mode_shape, correction, owner, panel)
    halo = exchange(edges)
    far = bits_of("gy")[::-1]
    where = gathered(far, mode_shape.shape[0])
    pieces = gather_step([weighted], "gy", far[0])
    field, *edges = sweep(False, coupling, omega, pressure_coef, state, right_side, sigma, halo)
    edges, pieces = lax.optimization_barrier((edges, pieces))
    halo = exchange(edges)
    for bit in far[1:-1]:
        pieces = gather_step(pieces, "gy", bit)
    field, table, press = sweep(True, coupling, omega, pressure_coef, field, right_side, sigma, halo)
    table, pieces = lax.optimization_barrier((table, pieces))
    pieces = gather_step(pieces, "gy", far[-1])
    keep, send = tile_sums(
        place.reshape(tiles), table, press, tile_cells, interp, panel_tiles * lax.axis_size("gy"), parts
    )
    send, pieces = lax.optimization_barrier((send, pieces))
    chunk = reduce_panels(keep, send, pieces, where)
    total = [chunk] + [swap(chunk, "gx", relative) for relative in range(1, lax.axis_size("gx"))]
    share = mode_shape.shape[0] // lax.axis_size("gy")
    panels, gaf = local_call(
        finish_kernel,
        ((parts, correction.shape[0]), (share, parts)),
        "finish",
        *total,
        scratch=(pltpu.VMEM((LANES, parts), F32),),
    )
    return (field, panels, gaf)


def solution(mesh):
    placed = (
        P(None, "gx", "gy"),
        P(None, "gx", "gy"),
        P("gx", "gy"),
        P(),
        P(),
        P(),
        P(("gx", "gy"), None),
        P(("gx", "gy"), None),
        P(("gx", "gy"), None),
        P(("gx", "gy"), None, None),
        P("gy"),
        P(None, "gy"),
    )
    return jax.shard_map(
        body,
        mesh=mesh,
        in_specs=placed,
        out_specs=(P(None, "gx", "gy"), P(None, "gy"), P("gy", None)),
        check_vma=False,
    )
```

```python
import functools

import jax
import jax.numpy as jnp
from jax import lax
from jax.experimental import pallas as pl
from jax.experimental.pallas import tpu as pltpu
from jax.sharding import PartitionSpec as P

F32 = jnp.float32
BF16 = jnp.bfloat16
LANES = 128
BLOCK_TILES = 32
LANE_TILES = 10
VMEM_LIMIT = 40 << 20
VMEM_ALL = 60 << 20
VMEM_SWEEP = 46 << 20
VMEM_SMALL = 12 << 20


def vmem():
    return pl.BlockSpec(memory_space=pltpu.VMEM)


def smem():
    return pl.BlockSpec(memory_space=pltpu.SMEM)


def pack_edges(field_ref, first, planes, row1_ref, row2_ref, col1_ref, col2_ref):
    rows, cols = field_ref.shape[1:]
    even_x = lax.rem(lax.axis_index("gx"), 2) == 0
    even_y = lax.rem(lax.axis_index("gy"), 2) == 0
    lane = lax.broadcasted_iota(jnp.int32, (rows, LANES), 1)
    left = jnp.where(even_y, col2_ref[...], col1_ref[...])
    right = jnp.where(even_y, col1_ref[...], col2_ref[...])
    for k in range(planes):
        row1_ref[0, k : k + 1, :] = field_ref[k, 0:1, :]
        row2_ref[0, k : k + 1, :] = field_ref[k, rows - 1 : rows, :]
        here = lane == first + k
        left = jnp.where(here, field_ref[k, :, 0:1], left)
        right = jnp.where(here, field_ref[k, :, cols - 1 : cols], right)
    col1_ref[...] = jnp.where(even_y, right, left)
    col2_ref[...] = jnp.where(even_y, left, right)
    up = row1_ref[0]
    down = row2_ref[0]
    row1_ref[0] = jnp.where(even_x, down, up)
    row2_ref[0] = jnp.where(even_x, up, down)


def pack_kernel(
    modes,
    state_ref,
    shape_ref,
    correction_ref,
    owner_ref,
    panel_ref,
    row1_ref,
    row2_ref,
    col1_ref,
    col2_ref,
    weighted_ref,
    place_ref,
    held_ref,
    shapes_ref,
    factor_ref,
    tiles_ref,
    sems,
):
    planes = state_ref.shape[0] // modes
    share = weighted_ref.shape[1]
    copies = []
    for mode in range(modes):
        block = pl.ds(mode * planes, planes)
        copies.append(pltpu.make_async_copy(state_ref.at[block], held_ref.at[block], sems.at[mode]))
    mine = pl.ds(pl.multiple_of(lax.axis_index("gx") * share, LANES), share)
    copies.append(pltpu.make_async_copy(shape_ref.at[:, mine], shapes_ref, sems.at[modes]))
    copies.append(pltpu.make_async_copy(correction_ref.at[:, mine], factor_ref, sems.at[modes + 1]))
    copies.append(pltpu.make_async_copy(owner_ref, tiles_ref.at[0], sems.at[modes + 2]))
    copies.append(pltpu.make_async_copy(panel_ref, tiles_ref.at[1], sems.at[modes + 3]))
    for copy in copies:
        copy.start()
    col1_ref[...] = jnp.zeros_like(col1_ref)
    col2_ref[...] = jnp.zeros_like(col2_ref)
    for mode in range(modes):
        copies[mode].wait()
        here = pl.ds(mode, 1)
        block = pl.ds(mode * planes, planes)
        pack_edges(
            held_ref.at[block], mode * planes, planes, row1_ref.at[here], row2_ref.at[here], col1_ref, col2_ref
        )
    for copy in copies[modes:]:
        copy.wait()
    weighted_ref[...] = shapes_ref[...] * factor_ref[...]
    place_ref[...] = places(tiles_ref[0], tiles_ref[1], shape_ref.shape[1] // LANES)


def sweep_kernel(
    last,
    coupling_ref,
    omega_ref,
    coef_ref,
    state_ref,
    right_ref,
    sigma_ref,
    row1_ref,
    row2_ref,
    col1_ref,
    col2_ref,
    *rest,
):
    *outs, nbs0_ref, nbs1_ref, a0_ref, a1_ref, b0_ref, b1_ref, rhs_ref, new_ref, in_sems, out_sems = rest
    nbs_refs, a_refs, b_refs = (nbs0_ref, nbs1_ref), (a0_ref, a1_ref), (b0_ref, b1_ref)
    modes = omega_ref.shape[0]
    planes, rows, cols = nbs0_ref.shape
    nvar = planes // 2
    parts = 2 * modes
    blocks = [pl.ds(mode * planes, planes) for mode in range(modes)]
    fetches = [
        pltpu.make_async_copy(right_ref.at[block], rhs_ref.at[block], in_sems.at[mode])
        for mode, block in enumerate(blocks)
    ]
    for fetch in fetches:
        fetch.start()
    if last:
        field_ref, table_ref, press_ref = outs
        sends = [
            pltpu.make_async_copy(new_ref.at[block], field_ref.at[block], out_sems.at[mode])
            for mode, block in enumerate(blocks)
        ]
    else:
        new_ref, *edge_refs = outs
        edge_refs[2][...] = jnp.zeros_like(edge_refs[2])
        edge_refs[3][...] = jnp.zeros_like(edge_refs[3])

    even_x = lax.rem(lax.axis_index("gx"), 2) == 0
    even_y = lax.rem(lax.axis_index("gy"), 2) == 0
    west_cols = jnp.where(even_y, col2_ref[...], col1_ref[...])
    east_cols = jnp.where(even_y, col1_ref[...], col2_ref[...])
    row = lax.broadcasted_iota(jnp.int32, (rows, cols), 0)
    lane = lax.broadcasted_iota(jnp.int32, (rows, LANES), 1)

    def factors(mode):
        freq = omega_ref[mode]
        dval = 4.0 + sigma_ref[...]
        scale = 0.8 / (dval * dval + freq * freq)
        a_refs[mode % 2][...] = dval * scale
        b_refs[mode % 2][...] = freq * scale

    def neighbours(mode, k):
        nbs_ref = nbs_refs[mode % 2]
        comp = mode * planes + k
        plane = state_ref[comp]
        row1 = row1_ref[mode, k : k + 1, :]
        row2 = row2_ref[mode, k : k + 1, :]
        above = jnp.where(even_x, row2, row1)
        below = jnp.where(even_x, row1, row2)
        total = jnp.where(row == 0, above, pltpu.roll(plane, 1, 0))
        total = total + jnp.where(row == rows - 1, below, pltpu.roll(plane, rows - 1, 0))
        west = pltpu.roll(west_cols, (LANES - comp) % LANES, 1)
        east = pltpu.roll(east_cols, LANES - 1 - comp, 1)
        from_west = pltpu.roll(plane, 1, 1)
        from_east = pltpu.roll(plane, cols - 1, 1)
        nbs_ref[k, :, :LANES] = (
            total[:, :LANES] + jnp.where(lane == 0, west, from_west[:, :LANES]) + from_east[:, :LANES]
        )
        nbs_ref[k, :, cols - LANES :] = (
            total[:, cols - LANES :]
            + from_west[:, cols - LANES :]
            + jnp.where(lane == LANES - 1, east, from_east[:, cols - LANES :])
        )

    weight = [[coupling_ref[v, w] for w in range(nvar)] for v in range(nvar)]
    coef = [coef_ref[v] for v in range(nvar)]

    def strip(mode, step):
        here = slice(step * 8, step * 8 + 8)
        base = mode * planes
        nbs = [nbs_refs[mode % 2][k, here, :] for k in range(planes)]
        a = a_refs[mode % 2][here, :]
        b = b_refs[mode % 2][here, :]
        press_re = press_im = None
        for v in range(nvar):
            res_re = rhs_ref[base + v, here, :]
            res_im = rhs_ref[base + nvar + v, here, :]
            for w in range(nvar):
                res_re = res_re + weight[v][w] * nbs[w]
                res_im = res_im + weight[v][w] * nbs[nvar + w]
            new_re = 0.2 * state_ref[base + v, here, :] + a * res_re + b * res_im
            new_im = 0.2 * state_ref[base + nvar + v, here, :] + a * res_im - b * res_re
            new_ref[base + v, here, :] = new_re
            new_ref[base + nvar + v, here, :] = new_im
            if last:
                press_re = coef[v] * new_re if v == 0 else press_re + coef[v] * new_re
                press_im = coef[v] * new_im if v == 0 else press_im + coef[v] * new_im
        if last:
            for part, value in enumerate((press_re, press_im)):
                start = step * (8 * parts) + 2 * mode + part
                for half in range(cols // LANES):
                    piece = value[:, half * LANES : (half + 1) * LANES]
                    press_ref[half, pl.ds(start, 8, stride=parts), :] = piece

    factors(0)
    for k in range(planes):
        neighbours(0, k)
    steps = rows // 8
    for mode in range(modes):
        fetches[mode].wait()
        if mode + 1 < modes:
            factors(mode + 1)
        for step in range(steps):
            strip(mode, step)
            if mode + 1 < modes:
                for k in range(planes * step // steps, planes * (step + 1) // steps):
                    neighbours(mode + 1, k)
        if last:
            sends[mode].start()
        else:
            here = pl.ds(mode, 1)
            pack_edges(
                new_ref.at[blocks[mode]],
                mode * planes,
                planes,
                edge_refs[0].at[here],
                edge_refs[1].at[here],
                edge_refs[2],
                edge_refs[3],
            )
    if last:
        size = table_ref.shape[0] // 2
        for half in range(cols // LANES):
            whole = press_ref[half]
            high = whole.astype(BF16)
            span = slice(half * LANES, (half + 1) * LANES)
            table_ref[:size, span] = high
            table_ref[size:, span] = (whole - high.astype(F32)).astype(BF16)
        for send in sends:
            send.wait()


def edge_shapes(modes, planes, rows, cols):
    return (
        jax.ShapeDtypeStruct((modes, planes, cols), F32),
        jax.ShapeDtypeStruct((modes, planes, cols), F32),
        jax.ShapeDtypeStruct((rows, LANES), F32),
        jax.ShapeDtypeStruct((rows, LANES), F32),
    )


def pack(state, modes, mode_shape, correction, owner, panel):
    comp, rows, cols = state.shape
    shapes = edge_shapes(modes, comp // modes, rows, cols)
    share = (mode_shape.shape[0], mode_shape.shape[1] // lax.axis_size("gx"))
    hbm = pl.BlockSpec(memory_space=pltpu.HBM)
    return pl.pallas_call(
        functools.partial(pack_kernel, modes),
        out_shape=shapes + (jax.ShapeDtypeStruct(share, F32), jax.ShapeDtypeStruct(owner.shape, jnp.int32)),
        in_specs=[hbm] * 5,
        out_specs=(vmem(),) * 6,
        scratch_shapes=[
            pltpu.VMEM(state.shape, F32),
            pltpu.VMEM(share, F32),
            pltpu.VMEM((1, share[1]), F32),
            pltpu.VMEM((2,) + owner.shape, jnp.int32),
            pltpu.SemaphoreType.DMA((modes + 4,)),
        ],
        compiler_params=pltpu.CompilerParams(vmem_limit_bytes=VMEM_ALL),
        name="pack",
    )(state, mode_shape, correction[None, :], owner, panel)


def exchange(edges):
    got = []
    for axis, first, second in (("gx", edges[0], edges[1]), ("gy", edges[2], edges[3])):
        count = lax.axis_size(axis)
        got.append(swap(first, axis, 1))
        pairs = [(i, i + 1) for i in range(1, count - 1, 2)]
        got.append(lax.ppermute(second, axis, pairs + [(b, a) for a, b in pairs]))
    return got


def sweep(last, coupling, omega, coef, field, rhs, sigma, halo):
    comp, rows, cols = field.shape
    modes = omega.shape[0]
    planes = comp // modes
    hbm = pl.BlockSpec(memory_space=pltpu.HBM)
    if last:
        extra = (
            jax.ShapeDtypeStruct((4 * modes * rows, cols), BF16),
            jax.ShapeDtypeStruct((cols // LANES, 2 * modes * rows, LANES), F32),
        )
    else:
        extra = edge_shapes(modes, planes, rows, cols)
    plane = pltpu.VMEM((rows, cols), F32)
    return pl.pallas_call(
        functools.partial(sweep_kernel, last),
        out_shape=(jax.ShapeDtypeStruct(field.shape, F32),) + extra,
        in_specs=[smem(), smem(), smem(), vmem(), hbm] + [vmem()] * 5,
        out_specs=(hbm if last else vmem(),) + (vmem(),) * len(extra),
        scratch_shapes=[
            pltpu.VMEM((planes, rows, cols), F32),
            pltpu.VMEM((planes, rows, cols), F32),
            plane,
            plane,
            plane,
            plane,
            pltpu.VMEM(rhs.shape, F32),
            pltpu.VMEM(field.shape if last else (8, LANES), F32),
            pltpu.SemaphoreType.DMA((modes,)),
            pltpu.SemaphoreType.DMA((modes,)),
        ],
        compiler_params=pltpu.CompilerParams(vmem_limit_bytes=VMEM_SWEEP),
        cost_estimate=pl.CostEstimate(flops=8 * 10**9, bytes_accessed=12 * field.size, transcendentals=0),
        name="sweep",
    )(coupling, omega, coef, field, rhs, sigma, *halo)


def tile_kernel(place_ref, table_ref, press_ref, cells_ref, interp_ref, keep_ref, send_ref, acc_ref):
    step = pl.program_id(0)
    block = cells_ref.shape[0]
    parts = acc_ref.shape[1]
    size = table_ref.shape[0] // 2
    cols = table_ref.shape[1]
    rows = size // parts
    shift = cols.bit_length() - 1

    @pl.when(step == 0)
    def _():
        acc_ref[...] = jnp.zeros_like(acc_ref)

    col_at = lax.broadcasted_iota(jnp.int16, (cols, 2 * LANES), 0)
    one = jnp.ones((), BF16)
    zero = jnp.zeros((), BF16)
    blank = jnp.zeros((2 * parts, LANES), F32)

    def by_matmul(pair):
        cells = jnp.concatenate(
            [cells_ref[2 * pair : 2 * pair + 1, :], cells_ref[2 * pair + 1 : 2 * pair + 2, :]], axis=1
        )
        col = jnp.broadcast_to((cells & (cols - 1)).astype(jnp.int16), (cols, 2 * LANES))
        hot = jnp.where(col_at == col, one, zero)
        found = jnp.dot(table_ref[...], hot, preferred_element_type=F32)
        found = (found[:size] + found[size:]).reshape(rows, parts, 2 * LANES)
        row = jnp.broadcast_to(cells >> shift, (parts, 2 * LANES))
        bit = rows // 2
        while bit:
            found = jnp.where(((row & bit) != 0)[None], found[bit:], found[:bit])
            bit //= 2
        return found[0]

    halves = cols // LANES
    lane_bits = LANES.bit_length() - 1

    def by_lanes(tile):
        cells = jnp.broadcast_to(cells_ref[tile : tile + 1, :], (parts, LANES))
        lane = cells & (LANES - 1)
        chosen = [(cells >> (lane_bits + b)) & 1 == 1 for b in range((rows * halves).bit_length() - 1)]

        def among(base, bits):
            if bits == 0:
                at = base // halves * parts
                return jnp.take_along_axis(press_ref[base % halves, at : at + parts, :], lane, axis=1)
            low = among(base, bits - 1)
            return jnp.where(chosen[bits - 1], among(base + (1 << (bits - 1)), bits - 1), low)

        return among(0, len(chosen))

    by_lane_count = LANE_TILES * block // BLOCK_TILES // 2 * 2
    pairs = (block - by_lane_count) // 2
    surfs = []
    beside = []
    for pair in range(pairs):
        for tile in range(pair * by_lane_count // pairs, (pair + 1) * by_lane_count // pairs):
            beside.append(by_lanes(block - by_lane_count + tile))
        surfs.append(by_matmul(pair))
    for pair in range(by_lane_count // 2):
        surfs.append(jnp.concatenate(beside[2 * pair : 2 * pair + 2], axis=1))
    for pair, surf in enumerate(surfs):
        high = surf.astype(BF16).astype(F32)
        split = jnp.concatenate([high, surf - high], axis=0)
        left = jnp.concatenate(
            [
                jnp.concatenate([split[:, :LANES], blank], axis=1),
                jnp.concatenate([blank, split[:, LANES:]], axis=1),
            ],
            axis=0,
        ).astype(BF16)
        weight = interp_ref[2 * pair : 2 * pair + 2].reshape(2 * LANES, LANES)
        weight_high = weight.astype(BF16)
        weight_low = (weight - weight_high.astype(F32)).astype(BF16)
        right = jnp.concatenate([weight_high, weight_low], axis=1)
        out = jnp.dot(left, right, preferred_element_type=F32)
        for side in range(2):
            line = out[side * 2 * parts : (side + 1) * 2 * parts]
            high_part = line[:parts, :LANES] + line[:parts, LANES:]
            at = place_ref[step * block + 2 * pair + side]
            acc_ref[at] += high_part + line[parts:, :LANES]

    @pl.when(step == pl.num_programs(0) - 1)
    def _():
        half = keep_ref.shape[0]
        keep_ref[...] = acc_ref[:half]
        send_ref[...] = acc_ref[half:]


def tile_sums(place, table, press, cells, interp, panel_tiles, parts):
    tiles = cells.shape[0]
    half = (panel_tiles // 2, parts, LANES)
    block = min(BLOCK_TILES, tiles)
    return pl.pallas_call(
        tile_kernel,
        grid=(tiles // block,),
        out_shape=(jax.ShapeDtypeStruct(half, F32), jax.ShapeDtypeStruct(half, F32)),
        in_specs=[
            smem(),
            pl.BlockSpec(table.shape, lambda i: (0, 0)),
            pl.BlockSpec(press.shape, lambda i: (0, 0, 0)),
            pl.BlockSpec((block, LANES), lambda i: (i, 0)),
            pl.BlockSpec((block, LANES, LANES), lambda i: (i, 0, 0)),
        ],
        out_specs=(pl.BlockSpec(half, lambda i: (0, 0, 0)), pl.BlockSpec(half, lambda i: (0, 0, 0))),
        scratch_shapes=[pltpu.VMEM((panel_tiles, parts, LANES), F32)],
        compiler_params=pltpu.CompilerParams(vmem_limit_bytes=VMEM_LIMIT),
        cost_estimate=pl.CostEstimate(
            flops=2 * table.size * cells.size, bytes_accessed=4 * interp.size, transcendentals=0
        ),
        name="tiles",
    )(place, table, press, cells, interp)


def combine_kernel(order, where, keep_ref, got_ref, *refs):
    owners = len(order)
    chunk = keep_ref.shape[0] // owners
    parts = keep_ref.shape[1]
    pieces = 1 + max(piece for piece, _ in where.values())
    shape_refs, out_refs = refs[:pieces], refs[pieces:]
    modes = shape_refs[0].shape[0]
    tiles = out_refs[0].shape[0] - 1
    force = jnp.zeros((parts, modes), F32)
    for at, relative in enumerate(order):
        first = at * chunk
        lines = keep_ref[first : first + chunk] + got_ref[first : first + chunk]
        out_refs[first // tiles][first % tiles : first % tiles + chunk] = lines
        force = force + lax.dot_general(
            jnp.concatenate([lines[k] for k in range(chunk)], axis=1),
            shape_refs[where[relative][0]][where[relative][1] : where[relative][1] + modes, :],
            (((1,), (1,)), ((), ())),
            precision=lax.Precision.HIGHEST,
            preferred_element_type=F32,
        )
    tile = jnp.concatenate([force, jnp.zeros((parts, LANES - modes), F32)], axis=1)
    for out_ref in out_refs:
        out_ref[tiles] = tile


def fold_kernel(count, *refs):
    total = refs[0][...]
    for ref in refs[1:count]:
        total = total + ref[...]
    tiles = refs[count].shape[0] - 1
    for number, ref in enumerate(refs[count:]):
        ref[:tiles] = total[number * tiles : (number + 1) * tiles]
        ref[tiles] = total[total.shape[0] - 1]


def finish_kernel(*refs):
    *total_refs, panel_ref, gaf_ref, turned_ref = refs
    chunk, parts, lanes = total_refs[0].shape
    chunk = chunk - 1
    here = lax.axis_index("gx")
    force = total_refs[0][chunk]
    for relative, total_ref in enumerate(total_refs):
        first = (here ^ relative) * (chunk * lanes)
        for k in range(chunk):
            panel_ref[:, pl.ds(pl.multiple_of(first + k * lanes, lanes), lanes)] = total_ref[k]
        if relative:
            force = force + total_ref[chunk]
    turned_ref[...] = jnp.transpose(force)
    share = gaf_ref.shape[0]
    gaf_ref[...] = turned_ref[pl.ds(lax.axis_index("gy") * share, share), :]


def local_call(kernel, shapes, name, *args, scratch=(), scalars=0):
    return pl.pallas_call(
        kernel,
        out_shape=tuple(jax.ShapeDtypeStruct(shape, F32) for shape in shapes),
        in_specs=[smem()] * scalars + [vmem()] * (len(args) - scalars),
        out_specs=tuple(vmem() for _ in shapes),
        scratch_shapes=list(scratch),
        compiler_params=pltpu.CompilerParams(vmem_limit_bytes=VMEM_SMALL),
        name=name,
    )(*args)


def reversed_bits(value, count):
    out = jnp.zeros_like(value)
    for bit in range(count.bit_length() - 1):
        out = out * 2 + ((value >> bit) & 1)
    return out


def places(owner, panel, panel_tiles):
    nx = lax.axis_size("gx")
    ny = lax.axis_size("gy")
    chunk = panel_tiles // nx
    to_x = (panel >> (chunk.bit_length() - 1)) ^ lax.axis_index("gx")
    to_y = owner ^ lax.axis_index("gy")
    return (reversed_bits(to_x, nx) * ny + position(to_y, "gy")) * chunk + (panel & (chunk - 1))


def swap(send, axis, bit):
    return lax.ppermute(send, axis, [(i, i ^ bit) for i in range(lax.axis_size(axis))])


def gather_step(pieces, axis, bit):
    whole = pieces[0] if len(pieces) == 1 else jnp.concatenate(pieces, axis=0)
    return pieces + [swap(whole, axis, bit)]


def gathered(bits, size):
    laid = [0]
    where = {0: (0, 0)}
    for number, bit in enumerate(bits):
        for at, relative in enumerate(laid):
            where[relative ^ bit] = (number + 1, at * size)
        laid = laid + [relative ^ bit for relative in laid]
    return where


def bits_of(axis):
    return [1 << b for b in range(lax.axis_size(axis).bit_length() - 1)]


def levels(axis):
    found = []
    base = 1
    while base < lax.axis_size(axis):
        left = lax.axis_size(axis) // base
        size = 2 if left.bit_length() % 2 == 0 else 4
        found.append((base, size))
        base *= size
    return found


def position(relative, axis):
    at = 0
    for base, size in levels(axis):
        at = at * size + ((relative >> (base.bit_length() - 1)) & (size - 1))
    return at


def reduce_panels(keep, send, pieces, where):
    gx_bits = bits_of("gx")
    for bit in gx_bits[:-1]:
        got = swap(send, "gx", bit)
        half = keep.shape[0] // 2
        send = keep[half:] + got[half:]
        keep = keep[:half] + got[:half]
    got = swap(send, "gx", gx_bits[-1])
    owners = lax.axis_size("gy")
    order = sorted(range(owners), key=lambda relative: position(relative, "gy"))
    steps = levels("gy")
    tiles = keep.shape[0] // steps[0][1]
    lines = keep.shape[1:]
    held = local_call(
        functools.partial(combine_kernel, order, where),
        ((tiles + 1,) + lines,) * steps[0][1],
        "combine",
        keep,
        got,
        *pieces,
    )
    for number, (base, size) in enumerate(steps):
        held = [held[0]] + [swap(held[r], "gy", base * r) for r in range(1, size)]
        parts = steps[number + 1][1] if number + 1 < len(steps) else 1
        tiles = tiles // parts
        held = local_call(functools.partial(fold_kernel, size), ((tiles + 1,) + lines,) * parts, "fold", *held)
    return held[0]


def body(
    state,
    right_side,
    sigma,
    coupling,
    omega,
    pressure_coef,
    tile_cells,
    tile_owner,
    tile_panel,
    interp,
    correction,
    mode_shape,
):
    modes = omega.shape[0]
    parts = 2 * modes
    panel_tiles = correction.shape[0] // LANES
    tiles = tile_cells.shape[0]
    owner = tile_owner.reshape(tiles // LANES, LANES)
    panel = tile_panel.reshape(tiles // LANES, LANES)
    *edges, weighted, place = pack(state, modes, mode_shape, correction, owner, panel)
    halo = exchange(edges)
    far = bits_of("gy")[::-1]
    where = gathered(far, mode_shape.shape[0])
    pieces = gather_step([weighted], "gy", far[0])
    field, *edges = sweep(False, coupling, omega, pressure_coef, state, right_side, sigma, halo)
    edges, pieces = lax.optimization_barrier((edges, pieces))
    halo = exchange(edges)
    for bit in far[1:-1]:
        pieces = gather_step(pieces, "gy", bit)
    field, table, press = sweep(True, coupling, omega, pressure_coef, field, right_side, sigma, halo)
    table, pieces = lax.optimization_barrier((table, pieces))
    pieces = gather_step(pieces, "gy", far[-1])
    keep, send = tile_sums(
        place.reshape(tiles), table, press, tile_cells, interp, panel_tiles * lax.axis_size("gy"), parts
    )
    send, pieces = lax.optimization_barrier((send, pieces))
    chunk = reduce_panels(keep, send, pieces, where)
    total = [chunk] + [swap(chunk, "gx", relative) for relative in range(1, lax.axis_size("gx"))]
    share = mode_shape.shape[0] // lax.axis_size("gy")
    panels, gaf = local_call(
        finish_kernel,
        ((parts, correction.shape[0]), (share, parts)),
        "finish",
        *total,
        scratch=(pltpu.VMEM((LANES, parts), F32),),
    )
    return (field, panels, gaf)


def solution(mesh):
    placed = (
        P(None, "gx", "gy"),
        P(None, "gx", "gy"),
        P("gx", "gy"),
        P(),
        P(),
        P(),
        P(("gx", "gy"), None),
        P(("gx", "gy"), None),
        P(("gx", "gy"), None),
        P(("gx", "gy"), None, None),
        P("gy"),
        P(None, "gy"),
    )
    return jax.shard_map(
        body,
        mesh=mesh,
        in_specs=placed,
        out_specs=(P(None, "gx", "gy"), P(None, "gy"), P("gy", None)),
        check_vma=False,
    )
```
